32 devices in a mesh: groups: 2 (over x), latent: 16 (over z, y, core).
Axes of the slice: x: 2, y: 2, z: 4, core: 2. Of those that a mesh axis runs over, the one named last changes fastest.
Arguments:
- activations: bfloat16 [512, 2304], P(('groups', 'latent')), parts along dimension 0, may hold values from -6 to 6
- encoder: bfloat16 [4096, 2304], P(('groups', 'latent')), parts along dimension 0, may hold values from -0.125 to 0.125
- encoder_bias: float32 [4096], P(('groups', 'latent')), parts along dimension 0, may hold values from -3 to 3
- decoder: bfloat16 [4096, 2304], P(('groups', 'latent')), parts along dimension 0, may hold values from -0.125 to 0.125
- decoder_bias: float32 [4608], P('groups'), parts along dimension 0, may hold values from -3 to 3
- encoder_moment: float32 [4096, 2304], P(('groups', 'latent')), parts along dimension 0, may hold values from -0.375 to 0.375
- encoder_square: float32 [4096, 2304], P(('groups', 'latent')), parts along dimension 0, may hold values from 3.90625e-05 to 0.001171875
- decoder_moment: float32 [4096, 2304], P(('groups', 'latent')), parts along dimension 0, may hold values from -0.25 to 0.25
- decoder_square: float32 [4096, 2304], P(('groups', 'latent')), parts along dimension 0, may hold values from 3.90625e-05 to 0.001171875
Outputs:
- row_error: bfloat16 [512, 2304], P(('groups', 'latent')), parts along dimension 0
- encoder_next: bfloat16 [4096, 2304], P(('groups', 'latent')), parts along dimension 0
- decoder_next: bfloat16 [4096, 2304], P(('groups', 'latent')), parts along dimension 0
- encoder_moment_next: float32 [4096, 2304], P(('groups', 'latent')), parts along dimension 0
- encoder_square_next: float32 [4096, 2304], P(('groups', 'latent')), parts along dimension 0
- decoder_moment_next: float32 [4096, 2304], P(('groups', 'latent')), parts along dimension 0
- decoder_square_next: float32 [4096, 2304], P(('groups', 'latent')), parts along dimension 0
The draws below stay inside these ranges and needn't reach their ends.
There are 2 independent parts, one for each index of `groups`. The reference program is written for one: setup_inputs(seed, part) draws one part's arguments, and reference() takes and returns one part's arrays. A program takes and returns all parts, laid end to end along the dimension named above; each array names one. Nothing has to cross between parts.
All inputs are finite; a program needn't handle non-finite values.
Results may differ from the reference program's by a relative error of at most 0.01.
Values may be sent and summed in bfloat16 or wider, within the bound.
No kernel may reach another device: no remote copies, remote signals or barrier semaphores. Data moves between devices by JAX's collectives and lax.ppermute only.
A program may use at most 128 MiB of HBM per device.

```python
import math
import jax
import jax.numpy as jnp
from jax import lax

D = 2304
LATENTS = 2048
ROWS = 256


def block_levels(own_key, extent, shards, smallest, top_value):
    def one(dim, shards_of):
        steps = jax.random.uniform(jax.random.fold_in(jax.random.fold_in(own_key, 6), dim), (shards_of,), jnp.float32, smallest / len(shards), top_value / len(shards))
        return jnp.repeat(jnp.exp(steps), extent[dim] // shards_of).reshape((-1,) + (1,) * (len(extent) - dim - 1))

    level = one(*shards[0])
    for cut in shards[1:]:
        level = level * one(*cut)
    return level


def gaussian(stream_key, dims, deviation, reach, cuts=(), dtype=jnp.bfloat16):
    drawn = deviation * jax.random.normal(stream_key, dims, jnp.float32)
    if cuts:
        drawn = drawn * block_levels(stream_key, dims, cuts, -0.22, 0.18)
    return jnp.clip(drawn, -reach, reach).astype(dtype)


def setup_inputs(seed: int = 0, part: int = 0) -> dict:
    keys = jax.random.split(jax.random.key(seed), 10)
    own_keys = jax.random.split(jax.random.fold_in(keys[9], part), 10)
    return {
        "activations": gaussian(own_keys[0], (ROWS, D), 1.0, 6.0, ((0, 16),)),
        "encoder": gaussian(own_keys[1], (LATENTS, D), D ** -0.5, 0.125, ((0, 16),)),
        "encoder_bias": gaussian(own_keys[2], (LATENTS,), 0.5, 3.0, ((0, 16),), jnp.float32),
        "decoder": gaussian(own_keys[3], (LATENTS, D), LATENTS ** -0.5, 0.125, ((0, 16),)),
        "decoder_bias": gaussian(own_keys[4], (D,), 0.5, 3.0, (), jnp.float32),
        "encoder_moment": gaussian(own_keys[5], (LATENTS, D), (0.4 * ROWS ** -0.5), 0.375, ((0, 16),), jnp.float32),
        "encoder_square": jnp.clip(jnp.exp(math.log(0.001171875) - 3.4011974 * jax.random.uniform(own_keys[6], (LATENTS, D), jnp.float32) ** block_levels(own_keys[6], (LATENTS, D), ((0, 16),), -0.2, 0.2)), 3.9062499126885086e-05, 0.001171875),
        "decoder_moment": gaussian(own_keys[7], (LATENTS, D), (0.3 * ROWS ** -0.5), 0.25, ((0, 16),), jnp.float32),
        "decoder_square": jnp.clip(jnp.exp(math.log(0.001171875) - 3.4011974 * jax.random.uniform(own_keys[8], (LATENTS, D), jnp.float32) ** block_levels(own_keys[8], (LATENTS, D), ((0, 16),), -0.2, 0.2)), 3.9062499126885086e-05, 0.001171875),
    }


beta_first = 0.9
beta_second = 0.999
step_rate = 0.001
adam_epsilon = 1e-08

def inner_last(left, right):
    return lax.dot_general(left, right, (((1,), (1,)), ((), ())), preferred_element_type=jnp.float32)

def inner_first(left, right):
    return lax.dot_general(left, right, (((0,), (0,)), ((), ())), preferred_element_type=jnp.float32)

def adam_update(weight, grad, moment, square):
    moment_next = beta_first * moment + (1.0 - beta_first) * grad
    square_next = beta_second * square + (1.0 - beta_second) * grad * grad
    weight_next = (weight.astype(jnp.float32) - step_rate * moment_next / (jnp.sqrt(square_next) + adam_epsilon)).astype(jnp.bfloat16)
    return (weight_next, moment_next, square_next)

def reference(activations, encoder, encoder_bias, decoder, decoder_bias, encoder_moment, encoder_square, decoder_moment, decoder_square):
    centered = (activations.astype(jnp.float32) - decoder_bias).astype(jnp.bfloat16)
    codes = jnp.maximum(inner_last(centered, encoder) + encoder_bias, 0.0).astype(jnp.bfloat16)
    summed = jnp.dot(codes, decoder, preferred_element_type=jnp.float32)
    row_error = (summed - centered.astype(jnp.float32)).astype(jnp.bfloat16)
    signal = inner_last(row_error, decoder)
    delta = jnp.where(codes > 0, signal, 0.0).astype(jnp.bfloat16)
    decoder_grad = inner_first(codes, row_error) / ROWS
    encoder_grad = inner_first(delta, centered) / ROWS
    encoder_next, encoder_moment_next, encoder_square_next = adam_update(encoder, encoder_grad, encoder_moment, encoder_square)
    decoder_next, decoder_moment_next, decoder_square_next = adam_update(decoder, decoder_grad, decoder_moment, decoder_square)
    return (row_error, encoder_next, decoder_next, encoder_moment_next, encoder_square_next, decoder_moment_next, decoder_square_next)
```

```python
import jax
import jax.numpy as jnp
from jax import lax
from jax.sharding import PartitionSpec as P

beta_first = 0.9
beta_second = 0.999
step_rate = 0.001
adam_epsilon = 1e-08


def inner_last(left, right):
    return lax.dot_general(
        left, right, (((1,), (1,)), ((), ())), preferred_element_type=jnp.float32
    )


def inner_first(left, right):
    return lax.dot_general(
        left, right, (((0,), (0,)), ((), ())), preferred_element_type=jnp.float32
    )


def adam_update(weight, grad, moment, square):
    moment_next = beta_first * moment + (1.0 - beta_first) * grad
    square_next = beta_second * square + (1.0 - beta_second) * grad * grad
    weight_next = (
        weight.astype(jnp.float32)
        - step_rate * moment_next / (jnp.sqrt(square_next) + adam_epsilon)
    ).astype(jnp.bfloat16)
    return (weight_next, moment_next, square_next)


def to_chip(block, distance):
    size = lax.axis_size("latent")
    return lax.ppermute(
        block, "latent", [(i, i ^ (2 * distance)) for i in range(size)]
    )


def to_other_core(block):
    size = lax.axis_size("latent")
    return lax.ppermute(block, "latent", [(i, i ^ 1) for i in range(size)])


def body(
    activations,
    encoder,
    encoder_bias,
    decoder,
    decoder_bias,
    encoder_moment,
    encoder_square,
    decoder_moment,
    decoder_square,
):
    rows_here, width = activations.shape
    latents_here = encoder.shape[0]
    size = lax.axis_size("latent")
    chips = size // 2
    total_rows = rows_here * size

    row_blocks = [activations] + [to_chip(activations, k) for k in range(1, chips)]
    encoder_both = jnp.concatenate([encoder, to_other_core(encoder)], 0)
    decoder_both = jnp.concatenate([decoder, to_other_core(decoder)], 0)
    bias_both = jnp.concatenate([encoder_bias, to_other_core(encoder_bias)], 0)

    rows_core = jnp.concatenate(row_blocks, 0)
    centered = (rows_core.astype(jnp.float32) - decoder_bias).astype(jnp.bfloat16)
    codes = jnp.maximum(inner_last(centered, encoder_both) + bias_both, 0.0).astype(
        jnp.bfloat16
    )
    partial_sums = jnp.dot(codes, decoder_both, preferred_element_type=jnp.float32).astype(
        jnp.bfloat16
    )
    summed = partial_sums[:rows_here].astype(jnp.float32)
    arrived = [
        to_chip(partial_sums[k * rows_here : (k + 1) * rows_here], k) for k in range(1, chips)
    ]
    for block in arrived:
        summed = summed + block.astype(jnp.float32)
    row_error = (summed - centered[:rows_here].astype(jnp.float32)).astype(jnp.bfloat16)

    other_codes = to_other_core(codes[:, latents_here:])
    other_centered = to_other_core(centered)
    codes_all = jnp.concatenate([codes[:, :latents_here], other_codes], 0)
    centered_all = jnp.concatenate([centered, other_centered], 0)

    error_core = jnp.concatenate([row_error] + [to_chip(row_error, k) for k in range(1, chips)], 0)
    error_all = jnp.concatenate([error_core, to_other_core(error_core)], 0)

    decoder_grad = inner_first(codes_all, error_all) / total_rows
    signal = inner_last(error_all, decoder)
    delta = jnp.where(codes_all > 0, signal, 0.0).astype(jnp.bfloat16)
    encoder_grad = inner_first(delta, centered_all) / total_rows
    encoder_next, encoder_moment_next, encoder_square_next = adam_update(
        encoder, encoder_grad, encoder_moment, encoder_square
    )
    decoder_next, decoder_moment_next, decoder_square_next = adam_update(
        decoder, decoder_grad, decoder_moment, decoder_square
    )
    return (
        row_error,
        encoder_next,
        decoder_next,
        encoder_moment_next,
        encoder_square_next,
        decoder_moment_next,
        decoder_square_next,
    )


def solution(mesh):
    sharded = P(("groups", "latent"), None)
    return jax.shard_map(
        body,
        mesh=mesh,
        in_specs=(
            sharded,
            sharded,
            P(("groups", "latent")),
            sharded,
            P("groups"),
            sharded,
            sharded,
            sharded,
            sharded,
        ),
        out_specs=(sharded,) * 7,
        check_vma=False,
    )
```

```python
import jax
import jax.numpy as jnp
from jax import lax
from jax.sharding import PartitionSpec as P

beta_first = 0.9
beta_second = 0.999
step_rate = 0.001
adam_epsilon = 1e-08


def inner_last(left, right):
    return lax.dot_general(
        left, right, (((1,), (1,)), ((), ())), preferred_element_type=jnp.float32
    )


def inner_first(left, right):
    return lax.dot_general(
        left, right, (((0,), (0,)), ((), ())), preferred_element_type=jnp.float32
    )


def adam_update(weight, grad, moment, square):
    moment_next = beta_first * moment + (1.0 - beta_first) * grad
    square_next = beta_second * square + (1.0 - beta_second) * grad * grad
    weight_next = (
        weight.astype(jnp.float32)
        - step_rate * moment_next / (jnp.sqrt(square_next) + adam_epsilon)
    ).astype(jnp.bfloat16)
    return (weight_next, moment_next, square_next)


def swap_all(blocks):
    size = lax.axis_size("latent")
    groups = [list(range(core, size, 2)) for core in range(2)]
    return lax.all_to_all(
        blocks, "latent", split_axis=0, concat_axis=0, axis_index_groups=groups, tiled=False
    )


def to_other_core(block):
    size = lax.axis_size("latent")
    return lax.ppermute(block, "latent", [(i, i ^ 1) for i in range(size)])


def body(
    activations,
    encoder,
    encoder_bias,
    decoder,
    decoder_bias,
    encoder_moment,
    encoder_square,
    decoder_moment,
    decoder_square,
):
    rows_here, width = activations.shape
    latents_here = encoder.shape[0]
    size = lax.axis_size("latent")
    chips = size // 2
    total_rows = rows_here * size

    rows_core = swap_all(jnp.broadcast_to(activations, (chips, rows_here, width))).reshape(
        chips * rows_here, width
    )
    encoder_both = jnp.concatenate([encoder, to_other_core(encoder)], 0)
    decoder_both = jnp.concatenate([decoder, to_other_core(decoder)], 0)
    bias_both = jnp.concatenate([encoder_bias, to_other_core(encoder_bias)], 0)

    centered = (rows_core.astype(jnp.float32) - decoder_bias).astype(jnp.bfloat16)
    codes = jnp.maximum(inner_last(centered, encoder_both) + bias_both, 0.0).astype(
        jnp.bfloat16
    )
    partial_sums = jnp.dot(codes, decoder_both, preferred_element_type=jnp.float32).astype(
        jnp.bfloat16
    )
    arrived = swap_all(partial_sums.reshape(chips, rows_here, width))
    summed = jnp.sum(arrived.astype(jnp.float32), 0)
    centered_own = (activations.astype(jnp.float32) - decoder_bias).astype(jnp.bfloat16)
    row_error = (summed - centered_own.astype(jnp.float32)).astype(jnp.bfloat16)

    other_codes = to_other_core(codes[:, latents_here:])
    other_centered = to_other_core(centered)
    codes_all = jnp.concatenate([codes[:, :latents_here], other_codes], 0)
    centered_all = jnp.concatenate([centered, other_centered], 0)

    error_core = swap_all(jnp.broadcast_to(row_error, (chips, rows_here, width))).reshape(
        chips * rows_here, width
    )
    error_all = jnp.concatenate([error_core, to_other_core(error_core)], 0)

    decoder_grad = inner_first(codes_all, error_all) / total_rows
    signal = inner_last(error_all, decoder)
    delta = jnp.where(codes_all > 0, signal, 0.0).astype(jnp.bfloat16)
    encoder_grad = inner_first(delta, centered_all) / total_rows
    encoder_next, encoder_moment_next, encoder_square_next = adam_update(
        encoder, encoder_grad, encoder_moment, encoder_square
    )
    decoder_next, decoder_moment_next, decoder_square_next = adam_update(
        decoder, decoder_grad, decoder_moment, decoder_square
    )
    return (
        row_error,
        encoder_next,
        decoder_next,
        encoder_moment_next,
        encoder_square_next,
        decoder_moment_next,
        decoder_square_next,
    )


def solution(mesh):
    sharded = P(("groups", "latent"), None)
    return jax.shard_map(
        body,
        mesh=mesh,
        in_specs=(
            sharded,
            sharded,
            P(("groups", "latent")),
            sharded,
            P("groups"),
            sharded,
            sharded,
            sharded,
            sharded,
        ),
        out_specs=(sharded,) * 7,
        check_vma=False,
    )
```

```python
import jax
import jax.numpy as jnp
from jax import lax
from jax.sharding import PartitionSpec as P

beta_first = 0.9
beta_second = 0.999
step_rate = 0.001
adam_epsilon = 1e-08


def inner_last(left, right):
    return lax.dot_general(
        left, right, (((1,), (1,)), ((), ())), preferred_element_type=jnp.float32
    )


def inner_first(left, right):
    return lax.dot_general(
        left, right, (((0,), (0,)), ((), ())), preferred_element_type=jnp.float32
    )


def adam_update(weight, grad, moment, square):
    moment_next = beta_first * moment + (1.0 - beta_first) * grad
    square_next = beta_second * square + (1.0 - beta_second) * grad * grad
    weight_next = (
        weight.astype(jnp.float32)
        - step_rate * moment_next / (jnp.sqrt(square_next) + adam_epsilon)
    ).astype(jnp.bfloat16)
    return (weight_next, moment_next, square_next)


def to_chip(block, distance):
    size = lax.axis_size("latent")
    return lax.ppermute(
        block, "latent", [(i, i ^ (2 * distance)) for i in range(size)]
    )


def to_other_core(block):
    size = lax.axis_size("latent")
    return lax.ppermute(block, "latent", [(i, i ^ 1) for i in range(size)])


def gather_chips(block, chips):
    far = [to_chip(block, k) for k in range(2, chips, 2)]
    blocks = [block, to_chip(block, 1)]
    for one in far:
        blocks += [one, to_chip(one, 1)]
    return blocks


def sum_chips(blocks):
    pairs = []
    for k in range(0, len(blocks), 2):
        pairs.append(
            blocks[k].astype(jnp.float32)
            + to_chip(blocks[k + 1].astype(jnp.bfloat16), 1).astype(jnp.float32)
        )
    summed = pairs[0]
    for k, pair in enumerate(pairs[1:], 1):
        summed = summed + to_chip(pair.astype(jnp.bfloat16), 2 * k).astype(jnp.float32)
    return summed


def body(
    activations,
    encoder,
    encoder_bias,
    decoder,
    decoder_bias,
    encoder_moment,
    encoder_square,
    decoder_moment,
    decoder_square,
):
    rows_here, width = activations.shape
    latents_here = encoder.shape[0]
    size = lax.axis_size("latent")
    chips = size // 2
    total_rows = rows_here * size

    row_blocks = gather_chips(activations, chips)
    encoder_both = jnp.concatenate([encoder, to_other_core(encoder)], 0)
    decoder_both = jnp.concatenate([decoder, to_other_core(decoder)], 0)
    bias_both = jnp.concatenate([encoder_bias, to_other_core(encoder_bias)], 0)

    rows_core = jnp.concatenate(row_blocks, 0)
    centered = (rows_core.astype(jnp.float32) - decoder_bias).astype(jnp.bfloat16)
    codes = jnp.maximum(inner_last(centered, encoder_both) + bias_both, 0.0).astype(
        jnp.bfloat16
    )
    partial_sums = jnp.dot(codes, decoder_both, preferred_element_type=jnp.float32)
    summed = sum_chips(
        [partial_sums[k * rows_here : (k + 1) * rows_here] for k in range(chips)]
    )
    row_error = (summed - centered[:rows_here].astype(jnp.float32)).astype(jnp.bfloat16)

    other_codes = to_other_core(codes[:, latents_here:])
    other_centered = to_other_core(centered)
    codes_all = jnp.concatenate([codes[:, :latents_here], other_codes], 0)
    centered_all = jnp.concatenate([centered, other_centered], 0)

    error_core = jnp.concatenate(gather_chips(row_error, chips), 0)
    error_all = jnp.concatenate([error_core, to_other_core(error_core)], 0)

    decoder_grad = inner_first(codes_all, error_all) / total_rows
    signal = inner_last(error_all, decoder)
    delta = jnp.where(codes_all > 0, signal, 0.0).astype(jnp.bfloat16)
    encoder_grad = inner_first(delta, centered_all) / total_rows
    encoder_next, encoder_moment_next, encoder_square_next = adam_update(
        encoder, encoder_grad, encoder_moment, encoder_square
    )
    decoder_next, decoder_moment_next, decoder_square_next = adam_update(
        decoder, decoder_grad, decoder_moment, decoder_square
    )
    return (
        row_error,
        encoder_next,
        decoder_next,
        encoder_moment_next,
        encoder_square_next,
        decoder_moment_next,
        decoder_square_next,
    )


def solution(mesh):
    sharded = P(("groups", "latent"), None)
    return jax.shard_map(
        body,
        mesh=mesh,
        in_specs=(
            sharded,
            sharded,
            P(("groups", "latent")),
            sharded,
            P("groups"),
            sharded,
            sharded,
            sharded,
            sharded,
        ),
        out_specs=(sharded,) * 7,
        check_vma=False,
    )
```

```python
import functools

import jax
import jax.numpy as jnp
from jax import lax
from jax.experimental import pallas as pl
from jax.experimental.pallas import tpu as pltpu
from jax.sharding import PartitionSpec as P

beta_first = 0.9
beta_second = 0.999
step_rate = 0.001
adam_epsilon = 1e-08


def inner_last(left, right):
    return lax.dot_general(
        left, right, (((1,), (1,)), ((), ())), preferred_element_type=jnp.float32
    )


def update_kernel(
    columns,
    scale,
    codes_across,
    centered,
    *refs,
):
    errors = refs[:4]
    encoder, decoder = refs[4:6]
    moments_in = refs[6:10]
    outs = refs[10:16]
    error_all = refs[16]
    held_in = refs[17:21]
    held_out = refs[21:27]
    sem_in, sem_out = refs[27:]
    width = encoder.shape[1]
    tiles = width // columns

    def span(t):
        return pl.ds(t * columns, columns)

    def fetch(t, i):
        return pltpu.make_async_copy(
            moments_in[i].at[:, span(t)], held_in[i].at[:, span(t)], sem_in.at[t, i]
        )

    def write(t, i):
        return pltpu.make_async_copy(
            held_out[i].at[:, span(t)], outs[i].at[:, span(t)], sem_out.at[t, i]
        )

    for t in range(tiles):
        for i in range(4):
            fetch(t, i).start()
    start = 0
    for one in errors:
        error_all[pl.ds(start, one.shape[0]), :] = one[...]
        start += one.shape[0]
    codes_t = codes_across[...]
    signal = inner_last(decoder[...], error_all[...])
    delta_t = jnp.where(codes_t.astype(jnp.float32) > 0, signal, 0.0).astype(jnp.bfloat16)
    for t in range(tiles):
        at = span(t)
        for i in range(4):
            fetch(t, i).wait()
        for which, (left, right, weight) in enumerate(
            ((delta_t, centered, encoder), (codes_t, error_all, decoder))
        ):
            grad = jnp.dot(left, right[:, at], preferred_element_type=jnp.float32) * scale
            moment = beta_first * held_in[2 * which][:, at] + (1.0 - beta_first) * grad
            square = (
                beta_second * held_in[2 * which + 1][:, at] + (1.0 - beta_second) * grad * grad
            )
            held_out[3 * which][:, at] = (
                weight[:, at].astype(jnp.float32)
                - step_rate * moment / (jnp.sqrt(square) + adam_epsilon)
            ).astype(jnp.bfloat16)
            held_out[3 * which + 1][:, at] = moment
            held_out[3 * which + 2][:, at] = square
            for i in range(3 * which, 3 * which + 3):
                write(t, i).start()
    for t in range(tiles):
        for i in range(6):
            write(t, i).wait()


def update(total_rows, codes_across, centered, errors, weights, moments):
    latents, width = weights[0].shape
    rows = centered.shape[0]
    columns = next(c for c in (384, 256, 128, width) if width % c == 0)
    tiles = width // columns
    full = jax.ShapeDtypeStruct((latents, width), jnp.float32)
    half = jax.ShapeDtypeStruct((latents, width), jnp.bfloat16)
    vmem = pl.BlockSpec(memory_space=pltpu.VMEM)
    anywhere = pl.BlockSpec(memory_space=pl.ANY)
    wide = pltpu.VMEM((latents, width), jnp.float32)
    narrow = pltpu.VMEM((latents, width), jnp.bfloat16)
    return pl.pallas_call(
        functools.partial(update_kernel, columns, 1.0 / total_rows),
        out_shape=(half, full, full, half, full, full),
        in_specs=[vmem] * 8 + [anywhere] * 4,
        out_specs=[anywhere] * 6,
        scratch_shapes=[
            pltpu.VMEM((rows, width), jnp.bfloat16),
            wide,
            wide,
            wide,
            wide,
            narrow,
            wide,
            wide,
            narrow,
            wide,
            wide,
            pltpu.SemaphoreType.DMA((tiles, 4)),
            pltpu.SemaphoreType.DMA((tiles, 6)),
        ],
        compiler_params=pltpu.CompilerParams(vmem_limit_bytes=40 * 1024 * 1024),
        cost_estimate=pl.CostEstimate(
            flops=6 * latents * width * rows,
            bytes_accessed=44 * latents * width,
            transcendentals=4 * latents * width,
        ),
        name="update",
    )(codes_across, centered, *errors, *weights, *moments)


def to_chip(block, distance):
    size = lax.axis_size("latent")
    return lax.ppermute(
        block, "latent", [(i, i ^ (2 * distance)) for i in range(size)]
    )


def to_other_core(block):
    size = lax.axis_size("latent")
    return lax.ppermute(block, "latent", [(i, i ^ 1) for i in range(size)])


def gather_chips(block, chips):
    far = [to_chip(block, k) for k in reversed(range(2, chips, 2))]
    far_next = [to_chip(one, 1) for one in far]
    return [block] + far[::-1] + [to_chip(block, 1)] + far_next[::-1]


def body(
    activations,
    encoder,
    encoder_bias,
    decoder,
    decoder_bias,
    encoder_moment,
    encoder_square,
    decoder_moment,
    decoder_square,
):
    rows_here, width = activations.shape
    latents_here = encoder.shape[0]
    size = lax.axis_size("latent")
    chips = size // 2
    pairs = chips // 2
    total_rows = rows_here * size

    rows_core = jnp.concatenate(gather_chips(activations, chips), 0)
    encoder_both = jnp.concatenate([encoder, to_other_core(encoder)], 0)
    decoder_both = jnp.concatenate([decoder, to_other_core(decoder)], 0)
    bias_both = jnp.concatenate([encoder_bias, to_other_core(encoder_bias)], 0)

    centered = (rows_core.astype(jnp.float32) - decoder_bias).astype(jnp.bfloat16)
    codes = jnp.maximum(inner_last(centered, encoder_both) + bias_both, 0.0).astype(
        jnp.bfloat16
    )
    other_codes = to_other_core(codes[:, latents_here:])
    other_centered = to_other_core(centered)

    given = jnp.dot(
        codes[pairs * rows_here :], decoder_both, preferred_element_type=jnp.float32
    ).astype(jnp.bfloat16)
    summed = None
    for k in range(pairs):
        rows = slice(k * rows_here, (k + 1) * rows_here)
        pair = jnp.dot(
            codes[rows], decoder_both, preferred_element_type=jnp.float32
        ) + to_chip(given[rows], 1).astype(jnp.float32)
        if k:
            pair = to_chip(pair.astype(jnp.bfloat16), 2 * k).astype(jnp.float32)
        summed = pair if summed is None else summed + pair
    row_error = (summed - centered[:rows_here].astype(jnp.float32)).astype(jnp.bfloat16)

    errors = gather_chips(row_error, chips)
    near = [0, 1, pairs, pairs + 1]
    rest = [k for k in range(chips) if k not in near]
    near_error = jnp.concatenate([errors[k] for k in near], 0)
    rest_error = jnp.concatenate([errors[k] for k in rest], 0)

    def arranged(whole):
        return [whole[k * rows_here : (k + 1) * rows_here] for k in near + rest]

    codes_across = jnp.concatenate(
        arranged(codes[:, :latents_here]) + arranged(other_codes), 0
    ).T
    centered_all = jnp.concatenate(arranged(centered) + arranged(other_centered), 0)
    (
        encoder_next,
        encoder_moment_next,
        encoder_square_next,
        decoder_next,
        decoder_moment_next,
        decoder_square_next,
    ) = update(
        total_rows,
        codes_across,
        centered_all,
        (near_error, rest_error, to_other_core(near_error), to_other_core(rest_error)),
        (encoder, decoder),
        (encoder_moment, encoder_square, decoder_moment, decoder_square),
    )
    return (
        row_error,
        encoder_next,
        decoder_next,
        encoder_moment_next,
        encoder_square_next,
        decoder_moment_next,
        decoder_square_next,
    )


def solution(mesh):
    sharded = P(("groups", "latent"), None)
    return jax.shard_map(
        body,
        mesh=mesh,
        in_specs=(
            sharded,
            sharded,
            P(("groups", "latent")),
            sharded,
            P("groups"),
            sharded,
            sharded,
            sharded,
            sharded,
        ),
        out_specs=(sharded,) * 7,
        check_vma=False,
    )
```

```python
import functools

import jax
import jax.numpy as jnp
from jax import lax
from jax.experimental import pallas as pl
from jax.experimental.pallas import tpu as pltpu
from jax.sharding import PartitionSpec as P

beta_first = 0.9
beta_second = 0.999
step_rate = 0.001
adam_epsilon = 1e-08


def inner_last(left, right):
    return lax.dot_general(
        left, right, (((1,), (1,)), ((), ())), preferred_element_type=jnp.float32
    )


def update_kernel(columns, rows_total, codes_across, centered, *refs):
    blocks = len(refs) - 20
    errors, (encoder, decoder) = refs[:blocks], refs[blocks : blocks + 2]
    moments = refs[blocks + 2 : blocks + 6]
    outs = refs[blocks + 6 : blocks + 12]
    error_all, *held, sem = refs[blocks + 12 :]
    tiles = encoder.shape[1] // columns

    def write(t, i):
        at = pl.ds(t * columns, columns)
        return pltpu.make_async_copy(held[i].at[:, at], outs[i].at[:, at], sem.at[t, i])

    start = 0
    for one in errors:
        error_all[pl.ds(start, one.shape[0]), :] = one[...]
        start += one.shape[0]
    codes_t = codes_across[...]
    signal = inner_last(decoder[...], error_all[...])
    delta_t = jnp.where(codes_t.astype(jnp.float32) > 0, signal, 0.0).astype(jnp.bfloat16)
    first = (1.0 - beta_first) / rows_total
    second = (1.0 - beta_second) / (rows_total * rows_total)
    for t in range(tiles):
        at = pl.ds(t * columns, columns)
        for which, (left, right, weight) in enumerate(
            ((delta_t, centered, encoder), (codes_t, error_all, decoder))
        ):
            total = jnp.dot(left, right[:, at], preferred_element_type=jnp.float32)
            moment = beta_first * moments[2 * which][:, at] + first * total
            square = beta_second * moments[2 * which + 1][:, at] + second * (total * total)
            root = square * lax.rsqrt(square)
            held[3 * which][:, at] = (
                weight[:, at].astype(jnp.float32)
                - step_rate * moment * pl.reciprocal(root + adam_epsilon, approx=True)
            ).astype(jnp.bfloat16)
            held[3 * which + 1][:, at] = moment
            held[3 * which + 2][:, at] = square
            for i in range(3 * which, 3 * which + 3):
                write(t, i).start()
    for t in range(tiles):
        for i in range(6):
            write(t, i).wait()


def update(total_rows, codes_across, centered, errors, weights, moments):
    latents, width = weights[0].shape
    rows = centered.shape[0]
    columns = next(c for c in (256, 128, width) if width % c == 0)
    full = jax.ShapeDtypeStruct((latents, width), jnp.float32)
    half = jax.ShapeDtypeStruct((latents, width), jnp.bfloat16)
    vmem = pl.BlockSpec(memory_space=pltpu.VMEM)
    wide = pltpu.VMEM((latents, width), jnp.float32)
    narrow = pltpu.VMEM((latents, width), jnp.bfloat16)
    return pl.pallas_call(
        functools.partial(update_kernel, columns, float(total_rows)),
        out_shape=(half, full, full, half, full, full),
        in_specs=[vmem] * (len(errors) + 8),
        out_specs=[pl.BlockSpec(memory_space=pl.ANY)] * 6,
        scratch_shapes=[
            pltpu.VMEM((rows, width), jnp.bfloat16),
            narrow,
            wide,
            wide,
            narrow,
            wide,
            wide,
            pltpu.SemaphoreType.DMA((width // columns, 6)),
        ],
        compiler_params=pltpu.CompilerParams(vmem_limit_bytes=20 * 1024 * 1024 + 8 * rows * width),
        cost_estimate=pl.CostEstimate(
            flops=6 * latents * width * rows,
            bytes_accessed=44 * latents * width,
            transcendentals=4 * latents * width,
        ),
        name="update",
    )(codes_across, centered, *errors, *weights, *moments)


def to_chip(block, distance):
    size = lax.axis_size("latent")
    return lax.ppermute(
        block, "latent", [(i, i ^ (2 * distance)) for i in range(size)]
    )


def to_other_core(block):
    size = lax.axis_size("latent")
    return lax.ppermute(block, "latent", [(i, i ^ 1) for i in range(size)])


def gather_chips(block, chips):
    near = [block, to_chip(block, 2)]
    far = [to_chip(block, k) for k in range(4, chips, 2)]
    near = jnp.concatenate(near, 0)
    far = jnp.concatenate(far, 0)
    return [near, far, to_chip(near, 1), to_chip(far, 1)]


def body(
    activations,
    encoder,
    encoder_bias,
    decoder,
    decoder_bias,
    encoder_moment,
    encoder_square,
    decoder_moment,
    decoder_square,
):
    rows_here, width = activations.shape
    latents_here = encoder.shape[0]
    size = lax.axis_size("latent")
    chips = size // 2
    pairs = chips // 2
    total_rows = rows_here * size

    rows_core = jnp.concatenate(gather_chips(activations, chips), 0)
    encoder_both = jnp.concatenate([encoder, to_other_core(encoder)], 0)
    decoder_both = jnp.concatenate([decoder, to_other_core(decoder)], 0)
    bias_both = jnp.concatenate([encoder_bias, to_other_core(encoder_bias)], 0)

    centered = (rows_core.astype(jnp.float32) - decoder_bias).astype(jnp.bfloat16)
    codes = jnp.maximum(inner_last(centered, encoder_both) + bias_both, 0.0).astype(
        jnp.bfloat16
    )
    other_codes = to_other_core(codes[:, latents_here:])
    other_centered = to_other_core(centered)

    split = 2 * rows_here
    given = jnp.dot(
        codes[pairs * rows_here :], decoder_both, preferred_element_type=jnp.float32
    ).astype(jnp.bfloat16)

    def pair_sums(first, last):
        return jnp.dot(
            codes[first:last], decoder_both, preferred_element_type=jnp.float32
        ) + to_chip(given[first:last], 1).astype(jnp.float32)

    near = pair_sums(0, split)
    far = pair_sums(split, pairs * rows_here).astype(jnp.bfloat16)
    summed = near[:rows_here] + to_chip(near[rows_here:].astype(jnp.bfloat16), 2).astype(
        jnp.float32
    )
    for k in range(2, pairs):
        block = far[(k - 2) * rows_here : (k - 1) * rows_here]
        summed = summed + to_chip(block, 2 * k).astype(jnp.float32)
    row_error = (summed - centered[:rows_here].astype(jnp.float32)).astype(jnp.bfloat16)

    errors = gather_chips(row_error, chips)
    codes_across = jnp.concatenate([codes[:, :latents_here], other_codes], 0).T
    centered_all = jnp.concatenate([centered, other_centered], 0)
    (
        encoder_next,
        encoder_moment_next,
        encoder_square_next,
        decoder_next,
        decoder_moment_next,
        decoder_square_next,
    ) = update(
        total_rows,
        codes_across,
        centered_all,
        errors + [to_other_core(one) for one in errors],
        (encoder, decoder),
        (encoder_moment, encoder_square, decoder_moment, decoder_square),
    )
    return (
        row_error,
        encoder_next,
        decoder_next,
        encoder_moment_next,
        encoder_square_next,
        decoder_moment_next,
        decoder_square_next,
    )


def solution(mesh):
    sharded = P(("groups", "latent"), None)
    return jax.shard_map(
        body,
        mesh=mesh,
        in_specs=(
            sharded,
            sharded,
            P(("groups", "latent")),
            sharded,
            P("groups"),
            sharded,
            sharded,
            sharded,
            sharded,
        ),
        out_specs=(sharded,) * 7,
        check_vma=False,
    )
```

```python
import functools

import jax
import jax.numpy as jnp
from jax import lax
from jax.experimental import pallas as pl
from jax.experimental.pallas import tpu as pltpu
from jax.sharding import PartitionSpec as P

beta_first = 0.9
beta_second = 0.999
step_rate = 0.001
adam_epsilon = 1e-08


def inner_last(left, right):
    return lax.dot_general(
        left, right, (((1,), (1,)), ((), ())), preferred_element_type=jnp.float32
    )


def update_kernel(columns, rows_total, codes_across, centered, *refs):
    blocks = len(refs) - 20
    errors, (encoder, decoder) = refs[:blocks], refs[blocks : blocks + 2]
    moments = refs[blocks + 2 : blocks + 6]
    outs = refs[blocks + 6 : blocks + 12]
    error_all, *held, sem = refs[blocks + 12 :]
    tiles = encoder.shape[1] // columns

    def write(t, i):
        at = pl.ds(t * columns, columns)
        return pltpu.make_async_copy(held[i].at[:, at], outs[i].at[:, at], sem.at[t, i])

    start = 0
    for one in errors:
        error_all[pl.ds(start, one.shape[0]), :] = one[...]
        start += one.shape[0]
    codes_t = codes_across[...]
    signal = inner_last(decoder[...], error_all[...])
    delta_t = jnp.where(codes_t.astype(jnp.float32) > 0, signal, 0.0).astype(jnp.bfloat16)
    first = (1.0 - beta_first) / rows_total
    second = (1.0 - beta_second) / (rows_total * rows_total)
    for t in range(tiles):
        at = pl.ds(t * columns, columns)
        for which, (left, right, weight) in enumerate(
            ((delta_t, centered, encoder), (codes_t, error_all, decoder))
        ):
            total = jnp.dot(left, right[:, at], preferred_element_type=jnp.float32)
            moment = beta_first * moments[2 * which][:, at] + first * total
            square = beta_second * moments[2 * which + 1][:, at] + second * (total * total)
            root = square * lax.rsqrt(square)
            held[3 * which][:, at] = (
                weight[:, at].astype(jnp.float32)
                - step_rate * moment * pl.reciprocal(root + adam_epsilon, approx=True)
            ).astype(jnp.bfloat16)
            held[3 * which + 1][:, at] = moment
            held[3 * which + 2][:, at] = square
            for i in range(3 * which, 3 * which + 3):
                write(t, i).start()
    for t in range(tiles):
        for i in range(6):
            write(t, i).wait()


def update(total_rows, codes_across, centered, errors, weights, moments):
    latents, width = weights[0].shape
    rows = centered.shape[0]
    columns = next(c for c in (256, 128, width) if width % c == 0)
    full = jax.ShapeDtypeStruct((latents, width), jnp.float32)
    half = jax.ShapeDtypeStruct((latents, width), jnp.bfloat16)
    vmem = pl.BlockSpec(memory_space=pltpu.VMEM)
    wide = pltpu.VMEM((latents, width), jnp.float32)
    narrow = pltpu.VMEM((latents, width), jnp.bfloat16)
    return pl.pallas_call(
        functools.partial(update_kernel, columns, float(total_rows)),
        out_shape=(half, full, full, half, full, full),
        in_specs=[vmem] * (len(errors) + 8),
        out_specs=[pl.BlockSpec(memory_space=pl.ANY)] * 6,
        scratch_shapes=[
            pltpu.VMEM((rows, width), jnp.bfloat16),
            narrow,
            wide,
            wide,
            narrow,
            wide,
            wide,
            pltpu.SemaphoreType.DMA((width // columns, 6)),
        ],
        compiler_params=pltpu.CompilerParams(vmem_limit_bytes=20 * 1024 * 1024 + 8 * rows * width),
        cost_estimate=pl.CostEstimate(
            flops=6 * latents * width * rows,
            bytes_accessed=44 * latents * width,
            transcendentals=4 * latents * width,
        ),
        name="update",
    )(codes_across, centered, *errors, *weights, *moments)


def to_chip(block, distance):
    size = lax.axis_size("latent")
    return lax.ppermute(
        block, "latent", [(i, i ^ (2 * distance)) for i in range(size)]
    )


def to_other_core(block):
    size = lax.axis_size("latent")
    return lax.ppermute(block, "latent", [(i, i ^ 1) for i in range(size)])


def gather_chips(block, chips):
    far = []
    for k in range(4, chips, 4):
        far.append(to_chip(block, k))
        far.append(to_chip(far[-1], 2))
    near = jnp.concatenate([block, to_chip(block, 2)], 0)
    even = [near] + far
    return even + [to_chip(one, 1) for one in even]


def body(
    activations,
    encoder,
    encoder_bias,
    decoder,
    decoder_bias,
    encoder_moment,
    encoder_square,
    decoder_moment,
    decoder_square,
):
    rows_here, width = activations.shape
    latents_here = encoder.shape[0]
    size = lax.axis_size("latent")
    chips = size // 2
    pairs = chips // 2
    total_rows = rows_here * size

    rows_core = jnp.concatenate(gather_chips(activations, chips), 0)
    encoder_both = jnp.concatenate([encoder, to_other_core(encoder)], 0)
    decoder_both = jnp.concatenate([decoder, to_other_core(decoder)], 0)
    bias_both = jnp.concatenate([encoder_bias, to_other_core(encoder_bias)], 0)

    centered = (rows_core.astype(jnp.float32) - decoder_bias).astype(jnp.bfloat16)
    codes = jnp.maximum(inner_last(centered, encoder_both) + bias_both, 0.0).astype(
        jnp.bfloat16
    )
    other_codes = to_other_core(codes[:, latents_here:])
    other_centered = to_other_core(centered)

    split = 2 * rows_here
    given = jnp.dot(
        codes[pairs * rows_here :], decoder_both, preferred_element_type=jnp.float32
    ).astype(jnp.bfloat16)

    def pair_sums(first, last):
        return jnp.dot(
            codes[first:last], decoder_both, preferred_element_type=jnp.float32
        ) + to_chip(given[first:last], 1).astype(jnp.float32)

    far = [
        pair_sums(k * rows_here, (k + 1) * rows_here).astype(jnp.bfloat16)
        for k in range(2, pairs)
    ]
    near = pair_sums(0, split)
    summed = near[:rows_here] + to_chip(near[rows_here:].astype(jnp.bfloat16), 2).astype(
        jnp.float32
    )
    for k, block in enumerate(far, 2):
        summed = summed + to_chip(block, 2 * k).astype(jnp.float32)
    row_error = (summed - centered[:rows_here].astype(jnp.float32)).astype(jnp.bfloat16)

    row_error, other_codes, other_centered = lax.optimization_barrier(
        (row_error, other_codes, other_centered)
    )
    errors = gather_chips(row_error, chips)
    codes_across = jnp.concatenate([codes[:, :latents_here], other_codes], 0).T
    centered_all = jnp.concatenate([centered, other_centered], 0)
    (
        encoder_next,
        encoder_moment_next,
        encoder_square_next,
        decoder_next,
        decoder_moment_next,
        decoder_square_next,
    ) = update(
        total_rows,
        codes_across,
        centered_all,
        errors + [to_other_core(one) for one in errors],
        (encoder, decoder),
        (encoder_moment, encoder_square, decoder_moment, decoder_square),
    )
    return (
        row_error,
        encoder_next,
        decoder_next,
        encoder_moment_next,
        encoder_square_next,
        decoder_moment_next,
        decoder_square_next,
    )


def solution(mesh):
    sharded = P(("groups", "latent"), None)
    return jax.shard_map(
        body,
        mesh=mesh,
        in_specs=(
            sharded,
            sharded,
            P(("groups", "latent")),
            sharded,
            P("groups"),
            sharded,
            sharded,
            sharded,
            sharded,
        ),
        out_specs=(sharded,) * 7,
        check_vma=False,
    )
```

```python
import functools

import jax
import jax.numpy as jnp
from jax import lax
from jax.experimental import pallas as pl
from jax.experimental.pallas import tpu as pltpu
from jax.sharding import PartitionSpec as P

beta_first = 0.9
beta_second = 0.999
step_rate = 0.001
adam_epsilon = 1e-08


def inner_last(left, right):
    return lax.dot_general(
        left, right, (((1,), (1,)), ((), ())), preferred_element_type=jnp.float32
    )


def update_kernel(columns, rows_total, codes_across, centered, *refs):
    blocks = len(refs) - 20
    errors, (encoder, decoder) = refs[:blocks], refs[blocks : blocks + 2]
    moments = refs[blocks + 2 : blocks + 6]
    outs = refs[blocks + 6 : blocks + 12]
    error_all, *held, sem = refs[blocks + 12 :]
    tiles = encoder.shape[1] // columns

    def write(t, i):
        at = pl.ds(t * columns, columns)
        return pltpu.make_async_copy(held[i].at[:, at], outs[i].at[:, at], sem.at[t, i])

    start = 0
    for one in errors:
        error_all[pl.ds(start, one.shape[0]), :] = one[...]
        start += one.shape[0]
    codes_t = codes_across[...]
    signal = inner_last(decoder[...], error_all[...])
    delta_t = jnp.where(codes_t.astype(jnp.float32) > 0, signal, 0.0).astype(jnp.bfloat16)
    first = (1.0 - beta_first) / rows_total
    second = (1.0 - beta_second) / (rows_total * rows_total)
    for t in range(tiles):
        at = pl.ds(t * columns, columns)
        for which, (left, right, weight) in enumerate(
            ((delta_t, centered, encoder), (codes_t, error_all, decoder))
        ):
            total = jnp.dot(left, right[:, at], preferred_element_type=jnp.float32)
            moment = beta_first * moments[2 * which][:, at] + first * total
            square = beta_second * moments[2 * which + 1][:, at] + second * (total * total)
            root = square * lax.rsqrt(square)
            held[3 * which][:, at] = (
                weight[:, at].astype(jnp.float32)
                - step_rate * moment * pl.reciprocal(root + adam_epsilon, approx=True)
            ).astype(jnp.bfloat16)
            held[3 * which + 1][:, at] = moment
            held[3 * which + 2][:, at] = square
            for i in range(3 * which, 3 * which + 3):
                write(t, i).start()
    for t in range(tiles):
        for i in range(6):
            write(t, i).wait()


def update(total_rows, codes_across, centered, errors, weights, moments):
    latents, width = weights[0].shape
    rows = centered.shape[0]
    columns = next(c for c in (256, 128, width) if width % c == 0)
    full = jax.ShapeDtypeStruct((latents, width), jnp.float32)
    half = jax.ShapeDtypeStruct((latents, width), jnp.bfloat16)
    vmem = pl.BlockSpec(memory_space=pltpu.VMEM)
    wide = pltpu.VMEM((latents, width), jnp.float32)
    narrow = pltpu.VMEM((latents, width), jnp.bfloat16)
    return pl.pallas_call(
        functools.partial(update_kernel, columns, float(total_rows)),
        out_shape=(half, full, full, half, full, full),
        in_specs=[vmem] * (len(errors) + 8),
        out_specs=[pl.BlockSpec(memory_space=pl.ANY)] * 6,
        scratch_shapes=[
            pltpu.VMEM((rows, width), jnp.bfloat16),
            narrow,
            wide,
            wide,
            narrow,
            wide,
            wide,
            pltpu.SemaphoreType.DMA((width // columns, 6)),
        ],
        compiler_params=pltpu.CompilerParams(vmem_limit_bytes=20 * 1024 * 1024 + 8 * rows * width),
        cost_estimate=pl.CostEstimate(
            flops=6 * latents * width * rows,
            bytes_accessed=44 * latents * width,
            transcendentals=4 * latents * width,
        ),
        name="update",
    )(codes_across, centered, *errors, *weights, *moments)


def to_chip(block, distance):
    size = lax.axis_size("latent")
    return lax.ppermute(
        block, "latent", [(i, i ^ (2 * distance)) for i in range(size)]
    )


def to_other_core(block):
    size = lax.axis_size("latent")
    return lax.ppermute(block, "latent", [(i, i ^ 1) for i in range(size)])


def gather_chips(block, chips, after=None):
    quads = [[to_chip(block, q)] for q in range(4, chips, 4)]
    if after is not None:
        block, _ = lax.optimization_barrier((block, after))
    quads = [[block]] + quads
    for quad in quads:
        quad += [to_chip(quad[0], k) for k in range(1, 4)]
    return quads


def sum_chips(parts):
    def quad_sum(q):
        total = parts[q]
        for k in range(1, 4):
            sent = to_chip(parts[q + k].astype(jnp.bfloat16), k)
            total = total + sent.astype(jnp.float32)
        return total

    far = [quad_sum(q).astype(jnp.bfloat16) for q in range(4, len(parts), 4)]
    if far:
        far, own = lax.optimization_barrier((far, parts[:4]))
        parts = own + parts[4:]
    arrived = [to_chip(one, 4 * q) for q, one in enumerate(far, 1)]
    summed = sum(one.astype(jnp.float32) for one in arrived)
    return summed + quad_sum(0)


def body(
    activations,
    encoder,
    encoder_bias,
    decoder,
    decoder_bias,
    encoder_moment,
    encoder_square,
    decoder_moment,
    decoder_square,
):
    rows_here, width = activations.shape
    latents_here = encoder.shape[0]
    size = lax.axis_size("latent")
    chips = size // 2
    total_rows = rows_here * size

    other_bias = to_other_core(encoder_bias)
    bias_both = jnp.concatenate([encoder_bias, other_bias], 0)
    encoder_both = jnp.concatenate([encoder, to_other_core(encoder)], 0)
    decoder_both = jnp.concatenate([decoder, to_other_core(decoder)], 0)
    rows_core = jnp.concatenate(sum(gather_chips(activations, chips, other_bias), []), 0)

    centered = (rows_core.astype(jnp.float32) - decoder_bias).astype(jnp.bfloat16)
    codes = jnp.maximum(inner_last(centered, encoder_both) + bias_both, 0.0).astype(
        jnp.bfloat16
    )
    other_codes = to_other_core(codes[:, latents_here:])
    other_centered = to_other_core(centered)

    quad = 4 * rows_here
    far = jnp.dot(codes[quad:], decoder_both, preferred_element_type=jnp.float32)
    near = jnp.dot(codes[:quad], decoder_both, preferred_element_type=jnp.float32)
    summed = sum_chips(
        [
            part[start : start + rows_here]
            for part in (near, far)
            for start in range(0, part.shape[0], rows_here)
        ]
    )
    row_error = (summed - centered[:rows_here].astype(jnp.float32)).astype(jnp.bfloat16)

    row_error, other_codes, other_centered = lax.optimization_barrier(
        (row_error, other_codes, other_centered)
    )
    near, *far = gather_chips(row_error, chips)
    errors = [jnp.concatenate(near, 0)]
    for one in far:
        errors += [one[0], jnp.concatenate(one[1:], 0)]
    codes_across = jnp.concatenate([codes[:, :latents_here], other_codes], 0).T
    centered_all = jnp.concatenate([centered, other_centered], 0)
    (
        encoder_next,
        encoder_moment_next,
        encoder_square_next,
        decoder_next,
        decoder_moment_next,
        decoder_square_next,
    ) = update(
        total_rows,
        codes_across,
        centered_all,
        errors + [to_other_core(one) for one in errors],
        (encoder, decoder),
        (encoder_moment, encoder_square, decoder_moment, decoder_square),
    )
    return (
        row_error,
        encoder_next,
        decoder_next,
        encoder_moment_next,
        encoder_square_next,
        decoder_moment_next,
        decoder_square_next,
    )


def solution(mesh):
    sharded = P(("groups", "latent"), None)
    return jax.shard_map(
        body,
        mesh=mesh,
        in_specs=(
            sharded,
            sharded,
            P(("groups", "latent")),
            sharded,
            P("groups"),
            sharded,
            sharded,
            sharded,
            sharded,
        ),
        out_specs=(sharded,) * 7,
        check_vma=False,
    )
```

```python
import functools

import jax
import jax.numpy as jnp
from jax import lax
from jax.experimental import pallas as pl
from jax.experimental.pallas import tpu as pltpu
from jax.sharding import PartitionSpec as P

beta_first = 0.9
beta_second = 0.999
step_rate = 0.001
adam_epsilon = 1e-08


def inner_last(left, right):
    return lax.dot_general(
        left, right, (((1,), (1,)), ((), ())), preferred_element_type=jnp.float32
    )


def update_kernel(columns, block, rows_total, codes_across, centered, *refs):
    blocks = len(refs) - 20
    errors, (encoder, decoder) = refs[:blocks], refs[blocks : blocks + 2]
    moments = refs[blocks + 2 : blocks + 6]
    outs = refs[blocks + 6 : blocks + 12]
    error_all, *held, sem = refs[blocks + 12 :]
    tiles = encoder.shape[1] // columns

    def write(t, i):
        at = pl.ds(t * columns, columns)
        return pltpu.make_async_copy(held[i].at[:, at], outs[i].at[:, at], sem.at[t, i])

    start = 0
    for one in errors:
        for first in (0, block):
            for at in range(first, one.shape[0], 2 * block):
                error_all[pl.ds(start, block), :] = one[pl.ds(at, block), :]
                start += block
    first = (1.0 - beta_first) / rows_total
    second = (1.0 - beta_second) / (rows_total * rows_total)

    def advance(which, left, right, weight):
        for t in range(tiles):
            at = pl.ds(t * columns, columns)
            total = jnp.dot(left, right[:, at], preferred_element_type=jnp.float32)
            moment = beta_first * moments[2 * which][:, at] + first * total
            square = beta_second * moments[2 * which + 1][:, at] + second * (total * total)
            root = square * lax.rsqrt(square)
            held[3 * which][:, at] = (
                weight[:, at].astype(jnp.float32)
                - step_rate * moment * pl.reciprocal(root + adam_epsilon, approx=True)
            ).astype(jnp.bfloat16)
            held[3 * which + 1][:, at] = moment
            held[3 * which + 2][:, at] = square
            for i in range(3 * which, 3 * which + 3):
                write(t, i).start()

    codes_t = codes_across[...]
    advance(1, codes_t, error_all, decoder)
    signal = inner_last(decoder[...], error_all[...])
    delta_t = jnp.where(codes_t.astype(jnp.float32) > 0, signal, 0.0).astype(jnp.bfloat16)
    advance(0, delta_t, centered, encoder)
    for t in range(tiles):
        for i in range(6):
            write(t, i).wait()


def update(total_rows, codes_across, centered, errors, block, weights, moments):
    latents, width = weights[0].shape
    rows = centered.shape[0]
    columns = next(c for c in (256, 128, width) if width % c == 0)
    full = jax.ShapeDtypeStruct((latents, width), jnp.float32)
    half = jax.ShapeDtypeStruct((latents, width), jnp.bfloat16)
    vmem = pl.BlockSpec(memory_space=pltpu.VMEM)
    wide = pltpu.VMEM((latents, width), jnp.float32)
    narrow = pltpu.VMEM((latents, width), jnp.bfloat16)
    return pl.pallas_call(
        functools.partial(update_kernel, columns, block, float(total_rows)),
        out_shape=(half, full, full, half, full, full),
        in_specs=[vmem] * (len(errors) + 8),
        out_specs=[pl.BlockSpec(memory_space=pl.ANY)] * 6,
        scratch_shapes=[
            pltpu.VMEM((rows, width), jnp.bfloat16),
            narrow,
            wide,
            wide,
            narrow,
            wide,
            wide,
            pltpu.SemaphoreType.DMA((width // columns, 6)),
        ],
        compiler_params=pltpu.CompilerParams(vmem_limit_bytes=20 * 1024 * 1024 + 8 * rows * width),
        cost_estimate=pl.CostEstimate(
            flops=6 * latents * width * rows,
            bytes_accessed=44 * latents * width,
            transcendentals=4 * latents * width,
        ),
        name="update",
    )(codes_across, centered, *errors, *weights, *moments)


def to_chip(block, distance):
    size = lax.axis_size("latent")
    return lax.ppermute(
        block, "latent", [(i, i ^ (2 * distance)) for i in range(size)]
    )


def to_other_core(block):
    size = lax.axis_size("latent")
    return lax.ppermute(block, "latent", [(i, i ^ 1) for i in range(size)])


def gather_chips(block, chips):
    even = [block] + [to_chip(block, k) for k in range(2, chips, 2)]
    return even, [to_chip(one, 1) for one in even]


def body(
    activations,
    encoder,
    encoder_bias,
    decoder,
    decoder_bias,
    encoder_moment,
    encoder_square,
    decoder_moment,
    decoder_square,
):
    rows_here, width = activations.shape
    latents_here = encoder.shape[0]
    size = lax.axis_size("latent")
    chips = size // 2
    pairs = chips // 2
    total_rows = rows_here * size

    even, odd = gather_chips(activations, chips)
    rows_core = jnp.concatenate(even + odd, 0)
    encoder_both = jnp.concatenate([encoder, to_other_core(encoder)], 0)
    decoder_both = jnp.concatenate([decoder, to_other_core(decoder)], 0)
    bias_both = jnp.concatenate([encoder_bias, to_other_core(encoder_bias)], 0)

    centered = (rows_core.astype(jnp.float32) - decoder_bias).astype(jnp.bfloat16)
    codes = jnp.maximum(inner_last(centered, encoder_both) + bias_both, 0.0).astype(
        jnp.bfloat16
    )
    other_codes = to_other_core(codes[:, latents_here:])
    other_centered = to_other_core(centered)

    split = 2 * rows_here
    given = jnp.dot(
        codes[pairs * rows_here :], decoder_both, preferred_element_type=jnp.float32
    ).astype(jnp.bfloat16)

    def pair_sums(first, last):
        return jnp.dot(
            codes[first:last], decoder_both, preferred_element_type=jnp.float32
        ) + to_chip(given[first:last], 1).astype(jnp.float32)

    far = pair_sums(split, pairs * rows_here).astype(jnp.bfloat16)
    near = pair_sums(0, split)
    summed = near[:rows_here] + to_chip(near[rows_here:].astype(jnp.bfloat16), 2).astype(
        jnp.float32
    )
    for k in range(2, pairs):
        block = far[(k - 2) * rows_here : (k - 1) * rows_here]
        summed = summed + to_chip(block, 2 * k).astype(jnp.float32)
    row_error = (summed - centered[:rows_here].astype(jnp.float32)).astype(jnp.bfloat16)

    row_error, other_codes, other_centered = lax.optimization_barrier(
        (row_error, other_codes, other_centered)
    )
    even, odd = gather_chips(row_error, chips)
    errors = jnp.concatenate([one for both in zip(even, odd) for one in both], 0)
    codes_across = jnp.concatenate([codes[:, :latents_here], other_codes], 0).T
    centered_all = jnp.concatenate([centered, other_centered], 0)
    (
        encoder_next,
        encoder_moment_next,
        encoder_square_next,
        decoder_next,
        decoder_moment_next,
        decoder_square_next,
    ) = update(
        total_rows,
        codes_across,
        centered_all,
        (errors, to_other_core(errors)),
        rows_here,
        (encoder, decoder),
        (encoder_moment, encoder_square, decoder_moment, decoder_square),
    )
    return (
        row_error,
        encoder_next,
        decoder_next,
        encoder_moment_next,
        encoder_square_next,
        decoder_moment_next,
        decoder_square_next,
    )


def solution(mesh):
    sharded = P(("groups", "latent"), None)
    return jax.shard_map(
        body,
        mesh=mesh,
        in_specs=(
            sharded,
            sharded,
            P(("groups", "latent")),
            sharded,
            P("groups"),
            sharded,
            sharded,
            sharded,
            sharded,
        ),
        out_specs=(sharded,) * 7,
        check_vma=False,
    )
```

```python
import functools

import jax
import jax.numpy as jnp
from jax import lax
from jax.experimental import pallas as pl
from jax.experimental.pallas import tpu as pltpu
from jax.sharding import PartitionSpec as P

beta_first = 0.9
beta_second = 0.999
step_rate = 0.001
adam_epsilon = 1e-08


def inner_last(left, right):
    return lax.dot_general(
        left, right, (((1,), (1,)), ((), ())), preferred_element_type=jnp.float32
    )


def update_kernel(columns, rows_total, codes_across, centered, *refs):
    blocks = len(refs) - 20
    errors, (encoder, decoder) = refs[:blocks], refs[blocks : blocks + 2]
    moments = refs[blocks + 2 : blocks + 6]
    outs = refs[blocks + 6 : blocks + 12]
    error_all, *held, sem = refs[blocks + 12 :]
    tiles = encoder.shape[1] // columns

    def write(t, i):
        at = pl.ds(t * columns, columns)
        return pltpu.make_async_copy(held[i].at[:, at], outs[i].at[:, at], sem.at[t, i])

    start = 0
    for one in errors:
        error_all[pl.ds(start, one.shape[0]), :] = one[...]
        start += one.shape[0]
    first = (1.0 - beta_first) / rows_total
    second = (1.0 - beta_second) / (rows_total * rows_total)

    def advance(which, left, right, weight):
        for t in range(tiles):
            at = pl.ds(t * columns, columns)
            total = jnp.dot(left, right[:, at], preferred_element_type=jnp.float32)
            moment = beta_first * moments[2 * which][:, at] + first * total
            square = beta_second * moments[2 * which + 1][:, at] + second * (total * total)
            root = square * lax.rsqrt(square)
            held[3 * which][:, at] = (
                weight[:, at].astype(jnp.float32)
                - step_rate * moment * pl.reciprocal(root + adam_epsilon, approx=True)
            ).astype(jnp.bfloat16)
            held[3 * which + 1][:, at] = moment
            held[3 * which + 2][:, at] = square
            for i in range(3 * which, 3 * which + 3):
                write(t, i).start()

    codes_t = codes_across[...]
    advance(1, codes_t, error_all, decoder)
    signal = inner_last(decoder[...], error_all[...])
    delta_t = jnp.where(codes_t.astype(jnp.float32) > 0, signal, 0.0).astype(jnp.bfloat16)
    advance(0, delta_t, centered, encoder)
    for t in range(tiles):
        for i in range(6):
            write(t, i).wait()


def update(total_rows, codes_across, centered, errors, weights, moments):
    latents, width = weights[0].shape
    rows = centered.shape[0]
    columns = next(c for c in (256, 128, width) if width % c == 0)
    full = jax.ShapeDtypeStruct((latents, width), jnp.float32)
    half = jax.ShapeDtypeStruct((latents, width), jnp.bfloat16)
    vmem = pl.BlockSpec(memory_space=pltpu.VMEM)
    wide = pltpu.VMEM((latents, width), jnp.float32)
    narrow = pltpu.VMEM((latents, width), jnp.bfloat16)
    return pl.pallas_call(
        functools.partial(update_kernel, columns, float(total_rows)),
        out_shape=(half, full, full, half, full, full),
        in_specs=[vmem] * (len(errors) + 8),
        out_specs=[pl.BlockSpec(memory_space=pl.ANY)] * 6,
        scratch_shapes=[
            pltpu.VMEM((rows, width), jnp.bfloat16),
            narrow,
            wide,
            wide,
            narrow,
            wide,
            wide,
            pltpu.SemaphoreType.DMA((width // columns, 6)),
        ],
        compiler_params=pltpu.CompilerParams(vmem_limit_bytes=20 * 1024 * 1024 + 8 * rows * width),
        cost_estimate=pl.CostEstimate(
            flops=6 * latents * width * rows,
            bytes_accessed=44 * latents * width,
            transcendentals=4 * latents * width,
        ),
        name="update",
    )(codes_across, centered, *errors, *weights, *moments)


def to_chip(block, distance):
    size = lax.axis_size("latent")
    return lax.ppermute(
        block, "latent", [(i, i ^ (2 * distance)) for i in range(size)]
    )


def to_other_core(block):
    size = lax.axis_size("latent")
    return lax.ppermute(block, "latent", [(i, i ^ 1) for i in range(size)])


def chip_order(chips):
    even = [k for k in range(4, chips, 2) if k != 6] + [2, 6][: chips // 2 - 1]
    return [0] + [k for one in even for k in (one, one + 1)] + [1]


def gather_chips(block, chips):
    blocks = {0: block}
    for k in range(2, chips, 2):
        blocks[k] = to_chip(block, k)
    for k in range(0, chips, 2):
        blocks[k + 1] = to_chip(blocks[k], 1)
    return jnp.concatenate([blocks[k] for k in chip_order(chips)], 0)


def body(
    activations,
    encoder,
    encoder_bias,
    decoder,
    decoder_bias,
    encoder_moment,
    encoder_square,
    decoder_moment,
    decoder_square,
):
    rows_here, width = activations.shape
    latents_here = encoder.shape[0]
    size = lax.axis_size("latent")
    chips = size // 2
    pairs = chips // 2
    total_rows = rows_here * size

    rows_core = gather_chips(activations, chips)
    encoder_both = jnp.concatenate([encoder, to_other_core(encoder)], 0)
    decoder_both = jnp.concatenate([decoder, to_other_core(decoder)], 0)
    bias_both = jnp.concatenate([encoder_bias, to_other_core(encoder_bias)], 0)

    centered = (rows_core.astype(jnp.float32) - decoder_bias).astype(jnp.bfloat16)
    codes = jnp.maximum(inner_last(centered, encoder_both) + bias_both, 0.0).astype(
        jnp.bfloat16
    )
    other_codes = to_other_core(codes[:, latents_here:])
    other_centered = to_other_core(centered)

    order = chip_order(chips)

    def codes_of(wanted):
        starts = [order.index(k) * rows_here for k in wanted]
        return jnp.concatenate([codes[at : at + rows_here] for at in starts], 0)

    even = list(range(0, chips, 2))
    split = 2 * rows_here
    given = jnp.dot(
        codes_of([k + 1 for k in even]), decoder_both, preferred_element_type=jnp.float32
    ).astype(jnp.bfloat16)

    def pair_sums(first, last):
        return jnp.dot(
            codes_of(even[first // rows_here : last // rows_here]),
            decoder_both,
            preferred_element_type=jnp.float32,
        ) + to_chip(given[first:last], 1).astype(jnp.float32)

    far = pair_sums(split, pairs * rows_here).astype(jnp.bfloat16)
    near = pair_sums(0, split)
    summed = near[:rows_here] + to_chip(near[rows_here:].astype(jnp.bfloat16), 2).astype(
        jnp.float32
    )
    for k in range(2, pairs):
        block = far[(k - 2) * rows_here : (k - 1) * rows_here]
        summed = summed + to_chip(block, 2 * k).astype(jnp.float32)
    row_error = (summed - centered[:rows_here].astype(jnp.float32)).astype(jnp.bfloat16)

    row_error, other_codes, other_centered = lax.optimization_barrier(
        (row_error, other_codes, other_centered)
    )
    errors = gather_chips(row_error, chips)
    codes_across = jnp.concatenate([codes[:, :latents_here], other_codes], 0).T
    centered_all = jnp.concatenate([centered, other_centered], 0)
    (
        encoder_next,
        encoder_moment_next,
        encoder_square_next,
        decoder_next,
        decoder_moment_next,
        decoder_square_next,
    ) = update(
        total_rows,
        codes_across,
        centered_all,
        (errors, to_other_core(errors)),
        (encoder, decoder),
        (encoder_moment, encoder_square, decoder_moment, decoder_square),
    )
    return (
        row_error,
        encoder_next,
        decoder_next,
        encoder_moment_next,
        encoder_square_next,
        decoder_moment_next,
        decoder_square_next,
    )


def solution(mesh):
    sharded = P(("groups", "latent"), None)
    return jax.shard_map(
        body,
        mesh=mesh,
        in_specs=(
            sharded,
            sharded,
            P(("groups", "latent")),
            sharded,
            P("groups"),
            sharded,
            sharded,
            sharded,
            sharded,
        ),
        out_specs=(sharded,) * 7,
        check_vma=False,
    )
```

```python
import functools

import jax
import jax.numpy as jnp
from jax import lax
from jax.experimental import pallas as pl
from jax.experimental.pallas import tpu as pltpu
from jax.sharding import PartitionSpec as P

beta_first = 0.9
beta_second = 0.999
step_rate = 0.001
adam_epsilon = 1e-08


def inner_last(left, right):
    return lax.dot_general(
        left, right, (((1,), (1,)), ((), ())), preferred_element_type=jnp.float32
    )


def update_kernel(columns, rows_total, codes_across, centered, *refs):
    blocks = len(refs) - 20
    errors, (encoder, decoder) = refs[:blocks], refs[blocks : blocks + 2]
    moments = refs[blocks + 2 : blocks + 6]
    outs = refs[blocks + 6 : blocks + 12]
    error_all, *held, sem = refs[blocks + 12 :]
    tiles = encoder.shape[1] // columns
    part = min(32, encoder.shape[0])

    def write(t, i):
        at = pl.ds(t * columns, columns)
        return pltpu.make_async_copy(held[i].at[:, at], outs[i].at[:, at], sem.at[t, i])

    start = 0
    for one in errors:
        error_all[pl.ds(start, one.shape[0]), :] = one[...]
        start += one.shape[0]
    first = (1.0 - beta_first) / rows_total
    second = (1.0 - beta_second) / (rows_total * rows_total)

    def advance(which, left, right, weight):
        for t in range(tiles):
            at = pl.ds(t * columns, columns)
            total = jnp.dot(left, right[:, at], preferred_element_type=jnp.float32)
            for start in range(0, total.shape[0], part):
                some = (pl.ds(start, part), at)
                grad = total[start : start + part]
                moment = beta_first * moments[2 * which][some] + first * grad
                square = beta_second * moments[2 * which + 1][some] + second * (grad * grad)
                root = square * lax.rsqrt(square)
                held[3 * which][some] = (
                    weight[some].astype(jnp.float32)
                    - step_rate * moment * pl.reciprocal(root + adam_epsilon, approx=True)
                ).astype(jnp.bfloat16)
                held[3 * which + 1][some] = moment
                held[3 * which + 2][some] = square
            for i in range(3 * which, 3 * which + 3):
                write(t, i).start()

    codes_t = codes_across[...]
    advance(1, codes_t, error_all, decoder)
    signal = inner_last(decoder[...], error_all[...])
    delta_t = jnp.where(codes_t.astype(jnp.float32) > 0, signal, 0.0).astype(jnp.bfloat16)
    advance(0, delta_t, centered, encoder)
    for t in range(tiles):
        for i in range(6):
            write(t, i).wait()


def update(total_rows, codes_across, centered, errors, weights, moments):
    latents, width = weights[0].shape
    rows = centered.shape[0]
    columns = next(c for c in (256, 128, width) if width % c == 0)
    full = jax.ShapeDtypeStruct((latents, width), jnp.float32)
    half = jax.ShapeDtypeStruct((latents, width), jnp.bfloat16)
    vmem = pl.BlockSpec(memory_space=pltpu.VMEM)
    wide = pltpu.VMEM((latents, width), jnp.float32)
    narrow = pltpu.VMEM((latents, width), jnp.bfloat16)
    return pl.pallas_call(
        functools.partial(update_kernel, columns, float(total_rows)),
        out_shape=(half, full, full, half, full, full),
        in_specs=[vmem] * (len(errors) + 8),
        out_specs=[pl.BlockSpec(memory_space=pl.ANY)] * 6,
        scratch_shapes=[
            pltpu.VMEM((rows, width), jnp.bfloat16),
            narrow,
            wide,
            wide,
            narrow,
            wide,
            wide,
            pltpu.SemaphoreType.DMA((width // columns, 6)),
        ],
        compiler_params=pltpu.CompilerParams(vmem_limit_bytes=20 * 1024 * 1024 + 8 * rows * width),
        cost_estimate=pl.CostEstimate(
            flops=6 * latents * width * rows,
            bytes_accessed=44 * latents * width,
            transcendentals=4 * latents * width,
        ),
        name="update",
    )(codes_across, centered, *errors, *weights, *moments)


def to_chip(block, distance):
    size = lax.axis_size("latent")
    return lax.ppermute(
        block, "latent", [(i, i ^ (2 * distance)) for i in range(size)]
    )


def to_other_core(block):
    size = lax.axis_size("latent")
    return lax.ppermute(block, "latent", [(i, i ^ 1) for i in range(size)])


def gather_chips(block, chips):
    even = [block] + [to_chip(block, k) for k in range(2, chips, 2)]
    return even, [to_chip(one, 1) for one in even]


def in_turn(even, odd):
    return [one for both in zip(even, odd) for one in both]


def body(
    activations,
    encoder,
    encoder_bias,
    decoder,
    decoder_bias,
    encoder_moment,
    encoder_square,
    decoder_moment,
    decoder_square,
):
    rows_here, width = activations.shape
    latents_here = encoder.shape[0]
    size = lax.axis_size("latent")
    chips = size // 2
    total_rows = rows_here * size

    rows_core = jnp.concatenate(in_turn(*gather_chips(activations, chips)), 0)
    encoder_both = jnp.concatenate([encoder, to_other_core(encoder)], 0)
    decoder_both = jnp.concatenate([decoder, to_other_core(decoder)], 0)
    bias_both = jnp.concatenate([encoder_bias, to_other_core(encoder_bias)], 0)

    centered = (rows_core.astype(jnp.float32) - decoder_bias).astype(jnp.bfloat16)
    codes = jnp.maximum(inner_last(centered, encoder_both) + bias_both, 0.0).astype(
        jnp.bfloat16
    )
    other_codes = to_other_core(codes[:, latents_here:])
    other_centered = to_other_core(centered)

    partial_sums = jnp.dot(codes, decoder_both, preferred_element_type=jnp.float32)
    parts = [partial_sums[k * rows_here : (k + 1) * rows_here] for k in range(chips)]

    def pair_sums(first, last, after=None):
        given = jnp.concatenate(parts[first + 1 : last : 2], 0).astype(jnp.bfloat16)
        came = to_chip(given, 1)
        if after is not None:
            came, _ = lax.optimization_barrier((came, after))
        return [
            parts[k] + came[at * rows_here : (at + 1) * rows_here].astype(jnp.float32)
            for at, k in enumerate(range(first, last, 2))
        ]

    far = [one.astype(jnp.bfloat16) for one in pair_sums(4, chips)]
    own, near = pair_sums(0, 4, far)
    summed = own + to_chip(near.astype(jnp.bfloat16), 2).astype(jnp.float32)
    for k, one in enumerate(far, 2):
        summed = summed + to_chip(one, 2 * k).astype(jnp.float32)
    row_error = (summed - centered[:rows_here].astype(jnp.float32)).astype(jnp.bfloat16)

    row_error, other_codes, other_centered = lax.optimization_barrier(
        (row_error, other_codes, other_centered)
    )
    blocks = in_turn(*gather_chips(row_error, chips))
    errors = [jnp.concatenate(blocks[:4], 0), jnp.concatenate(blocks[4:], 0)]
    codes_across = jnp.concatenate([codes[:, :latents_here], other_codes], 0).T
    centered_all = jnp.concatenate([centered, other_centered], 0)
    (
        encoder_next,
        encoder_moment_next,
        encoder_square_next,
        decoder_next,
        decoder_moment_next,
        decoder_square_next,
    ) = update(
        total_rows,
        codes_across,
        centered_all,
        errors + [to_other_core(one) for one in errors],
        (encoder, decoder),
        (encoder_moment, encoder_square, decoder_moment, decoder_square),
    )
    return (
        row_error,
        encoder_next,
        decoder_next,
        encoder_moment_next,
        encoder_square_next,
        decoder_moment_next,
        decoder_square_next,
    )


def solution(mesh):
    sharded = P(("groups", "latent"), None)
    return jax.shard_map(
        body,
        mesh=mesh,
        in_specs=(
            sharded,
            sharded,
            P(("groups", "latent")),
            sharded,
            P("groups"),
            sharded,
            sharded,
            sharded,
            sharded,
        ),
        out_specs=(sharded,) * 7,
        check_vma=False,
    )
```

```python
import functools

import jax
import jax.numpy as jnp
from jax import lax
from jax.experimental import pallas as pl
from jax.experimental.pallas import tpu as pltpu
from jax.sharding import PartitionSpec as P

beta_first = 0.9
beta_second = 0.999
step_rate = 0.001
adam_epsilon = 1e-08


def inner_last(left, right):
    return lax.dot_general(
        left, right, (((1,), (1,)), ((), ())), preferred_element_type=jnp.float32
    )


def update_kernel(columns, rows_total, codes_across, centered, *refs):
    blocks = len(refs) - 20
    errors, (encoder, decoder) = refs[:blocks], refs[blocks : blocks + 2]
    moments = refs[blocks + 2 : blocks + 6]
    outs = refs[blocks + 6 : blocks + 12]
    error_all, *held, sem = refs[blocks + 12 :]
    tiles = encoder.shape[1] // columns
    part = min(32, encoder.shape[0])

    def write(t, i):
        at = pl.ds(t * columns, columns)
        return pltpu.make_async_copy(held[i].at[:, at], outs[i].at[:, at], sem.at[t, i])

    start = 0
    for one in errors:
        error_all[pl.ds(start, one.shape[0]), :] = one[...]
        start += one.shape[0]
    first = (1.0 - beta_first) / rows_total
    second = (1.0 - beta_second) / (rows_total * rows_total)

    def advance(which, left, right, weight):
        for t in range(tiles):
            at = pl.ds(t * columns, columns)
            total = jnp.dot(left, right[:, at], preferred_element_type=jnp.float32)
            for start in range(0, total.shape[0], part):
                some = (pl.ds(start, part), at)
                grad = total[start : start + part]
                moment = beta_first * moments[2 * which][some] + first * grad
                square = beta_second * moments[2 * which + 1][some] + second * (grad * grad)
                root = square * lax.rsqrt(square)
                held[3 * which][some] = (
                    weight[some].astype(jnp.float32)
                    - step_rate * moment * pl.reciprocal(root + adam_epsilon, approx=True)
                ).astype(jnp.bfloat16)
                held[3 * which + 1][some] = moment
                held[3 * which + 2][some] = square
            for i in range(3 * which, 3 * which + 3):
                write(t, i).start()

    codes_t = codes_across[...]
    advance(1, codes_t, error_all, decoder)
    signal = inner_last(decoder[...], error_all[...])
    delta_t = jnp.where(codes_t.astype(jnp.float32) > 0, signal, 0.0).astype(jnp.bfloat16)
    advance(0, delta_t, centered, encoder)
    for t in range(tiles):
        for i in range(6):
            write(t, i).wait()


def update(total_rows, codes_across, centered, errors, weights, moments):
    latents, width = weights[0].shape
    rows = centered.shape[0]
    columns = next(c for c in (256, 128, width) if width % c == 0)
    full = jax.ShapeDtypeStruct((latents, width), jnp.float32)
    half = jax.ShapeDtypeStruct((latents, width), jnp.bfloat16)
    vmem = pl.BlockSpec(memory_space=pltpu.VMEM)
    wide = pltpu.VMEM((latents, width), jnp.float32)
    narrow = pltpu.VMEM((latents, width), jnp.bfloat16)
    return pl.pallas_call(
        functools.partial(update_kernel, columns, float(total_rows)),
        out_shape=(half, full, full, half, full, full),
        in_specs=[vmem] * (len(errors) + 8),
        out_specs=[pl.BlockSpec(memory_space=pl.ANY)] * 6,
        scratch_shapes=[
            pltpu.VMEM((rows, width), jnp.bfloat16),
            narrow,
            wide,
            wide,
            narrow,
            wide,
            wide,
            pltpu.SemaphoreType.DMA((width // columns, 6)),
        ],
        compiler_params=pltpu.CompilerParams(vmem_limit_bytes=20 * 1024 * 1024 + 8 * rows * width),
        cost_estimate=pl.CostEstimate(
            flops=6 * latents * width * rows,
            bytes_accessed=44 * latents * width,
            transcendentals=4 * latents * width,
        ),
        name="update",
    )(codes_across, centered, *errors, *weights, *moments)


def to_chip(block, distance):
    size = lax.axis_size("latent")
    return lax.ppermute(
        block, "latent", [(i, i ^ (2 * distance)) for i in range(size)]
    )


def to_other_core(block):
    size = lax.axis_size("latent")
    return lax.ppermute(block, "latent", [(i, i ^ 1) for i in range(size)])


def gather_chips(block, chips):
    even = [block] + [to_chip(block, k) for k in range(2, chips, 2)]
    return even, [to_chip(one, 1) for one in even]


def in_turn(even, odd):
    return [one for both in zip(even, odd) for one in both]


def body(
    activations,
    encoder,
    encoder_bias,
    decoder,
    decoder_bias,
    encoder_moment,
    encoder_square,
    decoder_moment,
    decoder_square,
):
    rows_here, width = activations.shape
    latents_here = encoder.shape[0]
    size = lax.axis_size("latent")
    chips = size // 2
    total_rows = rows_here * size

    rows_core = jnp.concatenate(in_turn(*gather_chips(activations, chips)), 0)
    encoder_both = jnp.concatenate([encoder, to_other_core(encoder)], 0)
    decoder_both = jnp.concatenate([decoder, to_other_core(decoder)], 0)
    bias_both = jnp.concatenate([encoder_bias, to_other_core(encoder_bias)], 0)

    centered = (rows_core.astype(jnp.float32) - decoder_bias).astype(jnp.bfloat16)
    codes = jnp.maximum(inner_last(centered, encoder_both) + bias_both, 0.0).astype(
        jnp.bfloat16
    )
    other_codes = to_other_core(codes[:, latents_here:])
    other_centered = to_other_core(centered)

    quad = 4 * rows_here
    parts = []
    for rows in (slice(0, quad), slice(quad, None)):
        sums = jnp.dot(codes[rows], decoder_both, preferred_element_type=jnp.float32)
        parts += [sums[at : at + rows_here] for at in range(0, sums.shape[0], rows_here)]

    def pair_sums(first, last, after=None):
        given = jnp.concatenate(parts[first + 1 : last : 2], 0).astype(jnp.bfloat16)
        came = to_chip(given, 1)
        if after is not None:
            came, _ = lax.optimization_barrier((came, after))
        return [
            parts[k] + came[at * rows_here : (at + 1) * rows_here].astype(jnp.float32)
            for at, k in enumerate(range(first, last, 2))
        ]

    far = [one.astype(jnp.bfloat16) for one in pair_sums(4, chips)]
    own, near = pair_sums(0, 4, far)
    summed = own + to_chip(near.astype(jnp.bfloat16), 2).astype(jnp.float32)
    for k, one in enumerate(far, 2):
        summed = summed + to_chip(one, 2 * k).astype(jnp.float32)
    row_error = (summed - centered[:rows_here].astype(jnp.float32)).astype(jnp.bfloat16)

    row_error, other_codes, other_centered = lax.optimization_barrier(
        (row_error, other_codes, other_centered)
    )
    blocks = in_turn(*gather_chips(row_error, chips))
    errors = [jnp.concatenate(blocks, 0)]
    errors += [to_other_core(jnp.concatenate(one, 0)) for one in (blocks[:4], blocks[4:])]
    codes_across = jnp.concatenate([codes[:, :latents_here], other_codes], 0).T
    centered_all = jnp.concatenate([centered, other_centered], 0)
    (
        encoder_next,
        encoder_moment_next,
        encoder_square_next,
        decoder_next,
        decoder_moment_next,
        decoder_square_next,
    ) = update(
        total_rows,
        codes_across,
        centered_all,
        errors,
        (encoder, decoder),
        (encoder_moment, encoder_square, decoder_moment, decoder_square),
    )
    return (
        row_error,
        encoder_next,
        decoder_next,
        encoder_moment_next,
        encoder_square_next,
        decoder_moment_next,
        decoder_square_next,
    )


def solution(mesh):
    sharded = P(("groups", "latent"), None)
    return jax.shard_map(
        body,
        mesh=mesh,
        in_specs=(
            sharded,
            sharded,
            P(("groups", "latent")),
            sharded,
            P("groups"),
            sharded,
            sharded,
            sharded,
            sharded,
        ),
        out_specs=(sharded,) * 7,
        check_vma=False,
    )
```

```python
import functools

import jax
import jax.numpy as jnp
from jax import lax
from jax.experimental import pallas as pl
from jax.experimental.pallas import tpu as pltpu
from jax.sharding import PartitionSpec as P

beta_first = 0.9
beta_second = 0.999
step_rate = 0.001
adam_epsilon = 1e-08


def inner_last(left, right):
    return lax.dot_general(
        left, right, (((1,), (1,)), ((), ())), preferred_element_type=jnp.float32
    )


def update_kernel(columns, rows_total, codes_across, centered, *refs):
    blocks = len(refs) - 20
    errors, (encoder, decoder) = refs[:blocks], refs[blocks : blocks + 2]
    moments = refs[blocks + 2 : blocks + 6]
    outs = refs[blocks + 6 : blocks + 12]
    error_all, *held, sem = refs[blocks + 12 :]
    tiles = encoder.shape[1] // columns
    part = min(32, encoder.shape[0])

    def write(t, i):
        at = pl.ds(t * columns, columns)
        return pltpu.make_async_copy(held[i].at[:, at], outs[i].at[:, at], sem.at[t, i])

    start = 0
    for one in errors:
        error_all[pl.ds(start, one.shape[0]), :] = one[...]
        start += one.shape[0]
    first = (1.0 - beta_first) / rows_total
    second = (1.0 - beta_second) / (rows_total * rows_total)

    def advance(which, left, right, weight):
        for t in range(tiles):
            at = pl.ds(t * columns, columns)
            total = jnp.dot(left, right[:, at], preferred_element_type=jnp.float32)
            for start in range(0, total.shape[0], part):
                some = (pl.ds(start, part), at)
                grad = total[start : start + part]
                moment = moments[2 * which][some] + first * grad
                square = moments[2 * which + 1][some] + second * (grad * grad)
                root = square * lax.rsqrt(square)
                held[3 * which][some] = (
                    weight[some].astype(jnp.float32)
                    - step_rate * moment * pl.reciprocal(root + adam_epsilon, approx=True)
                ).astype(jnp.bfloat16)
                held[3 * which + 1][some] = moment
                held[3 * which + 2][some] = square
            for i in range(3 * which, 3 * which + 3):
                write(t, i).start()

    codes_t = codes_across[...]
    advance(1, codes_t, error_all, decoder)
    signal = inner_last(decoder[...], error_all[...])
    delta_t = jnp.where(codes_t.astype(jnp.float32) > 0, signal, 0.0).astype(jnp.bfloat16)
    advance(0, delta_t, centered, encoder)
    for t in range(tiles):
        for i in range(6):
            write(t, i).wait()


def update(total_rows, codes_across, centered, errors, weights, moments):
    latents, width = weights[0].shape
    rows = centered.shape[0]
    columns = next(c for c in (256, 128, width) if width % c == 0)
    full = jax.ShapeDtypeStruct((latents, width), jnp.float32)
    half = jax.ShapeDtypeStruct((latents, width), jnp.bfloat16)
    vmem = pl.BlockSpec(memory_space=pltpu.VMEM)
    wide = pltpu.VMEM((latents, width), jnp.float32)
    narrow = pltpu.VMEM((latents, width), jnp.bfloat16)
    return pl.pallas_call(
        functools.partial(update_kernel, columns, float(total_rows)),
        out_shape=(half, full, full, half, full, full),
        in_specs=[vmem] * (len(errors) + 8),
        out_specs=[pl.BlockSpec(memory_space=pl.ANY)] * 6,
        scratch_shapes=[
            pltpu.VMEM((rows, width), jnp.bfloat16),
            narrow,
            wide,
            wide,
            narrow,
            wide,
            wide,
            pltpu.SemaphoreType.DMA((width // columns, 6)),
        ],
        compiler_params=pltpu.CompilerParams(vmem_limit_bytes=20 * 1024 * 1024 + 8 * rows * width),
        cost_estimate=pl.CostEstimate(
            flops=6 * latents * width * rows,
            bytes_accessed=44 * latents * width,
            transcendentals=4 * latents * width,
        ),
        name="update",
    )(codes_across, centered, *errors, *weights, *moments)


def to_chip(block, distance):
    size = lax.axis_size("latent")
    return lax.ppermute(
        block, "latent", [(i, i ^ (2 * distance)) for i in range(size)]
    )


def to_other_core(block):
    size = lax.axis_size("latent")
    return lax.ppermute(block, "latent", [(i, i ^ 1) for i in range(size)])


def gather_chips(block, chips, before=None):
    even = [block] + [to_chip(block, k) for k in range(2, chips, 2)]
    if before is not None:
        even[2], before = lax.optimization_barrier((even[2], before))
    return even, [to_chip(one, 1) for one in even], before


def in_turn(even, odd):
    return [one for both in zip(even, odd) for one in both]


def body(
    activations,
    encoder,
    encoder_bias,
    decoder,
    decoder_bias,
    encoder_moment,
    encoder_square,
    decoder_moment,
    decoder_square,
):
    rows_here, width = activations.shape
    latents_here = encoder.shape[0]
    size = lax.axis_size("latent")
    chips = size // 2
    total_rows = rows_here * size

    decayed = (
        beta_first * encoder_moment,
        beta_second * encoder_square,
        beta_first * decoder_moment,
        beta_second * decoder_square,
    )
    even, odd, decayed = gather_chips(activations, chips, decayed)
    rows_core = jnp.concatenate(in_turn(even, odd), 0)
    encoder_both = jnp.concatenate([encoder, to_other_core(encoder)], 0)
    decoder_both = jnp.concatenate([decoder, to_other_core(decoder)], 0)
    bias_both = jnp.concatenate([encoder_bias, to_other_core(encoder_bias)], 0)

    centered = (rows_core.astype(jnp.float32) - decoder_bias).astype(jnp.bfloat16)
    codes = jnp.maximum(inner_last(centered, encoder_both) + bias_both, 0.0).astype(
        jnp.bfloat16
    )
    other_codes = to_other_core(codes[:, latents_here:])
    other_centered = to_other_core(centered)

    quad = 4 * rows_here
    parts = []
    for rows in (slice(0, quad), slice(quad, None)):
        sums = jnp.dot(codes[rows], decoder_both, preferred_element_type=jnp.float32)
        parts += [sums[at : at + rows_here] for at in range(0, sums.shape[0], rows_here)]

    def pair_sums(first, last, after=None):
        given = jnp.concatenate(parts[first + 1 : last : 2], 0).astype(jnp.bfloat16)
        came = to_chip(given, 1)
        if after is not None:
            came, _ = lax.optimization_barrier((came, after))
        return [
            parts[k] + came[at * rows_here : (at + 1) * rows_here].astype(jnp.float32)
            for at, k in enumerate(range(first, last, 2))
        ]

    far = [one.astype(jnp.bfloat16) for one in pair_sums(4, chips)]
    own, near = pair_sums(0, 4, far)
    summed = own + to_chip(near.astype(jnp.bfloat16), 2).astype(jnp.float32)
    for k, one in enumerate(far, 2):
        summed = summed + to_chip(one, 2 * k).astype(jnp.float32)
    row_error = (summed - centered[:rows_here].astype(jnp.float32)).astype(jnp.bfloat16)

    row_error, other_codes, other_centered = lax.optimization_barrier(
        (row_error, other_codes, other_centered)
    )
    even, odd, _ = gather_chips(row_error, chips)
    blocks = in_turn(even, odd)
    errors = [jnp.concatenate(blocks, 0)]
    errors += [to_other_core(jnp.concatenate(one, 0)) for one in (blocks[:4], blocks[4:])]
    codes_across = jnp.concatenate([codes[:, :latents_here], other_codes], 0).T
    centered_all = jnp.concatenate([centered, other_centered], 0)
    (
        encoder_next,
        encoder_moment_next,
        encoder_square_next,
        decoder_next,
        decoder_moment_next,
        decoder_square_next,
    ) = update(
        total_rows,
        codes_across,
        centered_all,
        errors,
        (encoder, decoder),
        decayed,
    )
    return (
        row_error,
        encoder_next,
        decoder_next,
        encoder_moment_next,
        encoder_square_next,
        decoder_moment_next,
        decoder_square_next,
    )


def solution(mesh):
    sharded = P(("groups", "latent"), None)
    return jax.shard_map(
        body,
        mesh=mesh,
        in_specs=(
            sharded,
            sharded,
            P(("groups", "latent")),
            sharded,
            P("groups"),
            sharded,
            sharded,
            sharded,
            sharded,
        ),
        out_specs=(sharded,) * 7,
        check_vma=False,
    )
```

```python
import functools

import jax
import jax.numpy as jnp
from jax import lax
from jax.experimental import pallas as pl
from jax.experimental.pallas import tpu as pltpu
from jax.sharding import PartitionSpec as P

beta_first = 0.9
beta_second = 0.999
step_rate = 0.001
adam_epsilon = 1e-08


def inner_last(left, right):
    return lax.dot_general(
        left, right, (((1,), (1,)), ((), ())), preferred_element_type=jnp.float32
    )


def update_kernel(columns, rows_total, codes_across, centered, *refs):
    blocks = len(refs) - 20
    errors, (encoder, decoder) = refs[:blocks], refs[blocks : blocks + 2]
    moments = refs[blocks + 2 : blocks + 6]
    outs = refs[blocks + 6 : blocks + 12]
    error_all, *held, sem = refs[blocks + 12 :]
    tiles = encoder.shape[1] // columns
    part = min(32, encoder.shape[0])

    groups = next(n for n in (3, 1) if tiles % n == 0)
    wide = encoder.shape[1] // groups

    def write(group, i):
        at = pl.ds(group * wide, wide)
        return pltpu.make_async_copy(held[i].at[:, at], outs[i].at[:, at], sem.at[group, i])

    start = 0
    for one in errors:
        error_all[pl.ds(start, one.shape[0]), :] = one[...]
        start += one.shape[0]
    first = (1.0 - beta_first) / rows_total
    second = (1.0 - beta_second) / (rows_total * rows_total)

    def advance(which, left, right, weight):
        for t in range(tiles):
            at = pl.ds(t * columns, columns)
            total = jnp.dot(left, right[:, at], preferred_element_type=jnp.float32)
            for start in range(0, total.shape[0], part):
                some = (pl.ds(start, part), at)
                grad = total[start : start + part]
                moment = beta_first * moments[2 * which][some] + first * grad
                square = beta_second * moments[2 * which + 1][some] + second * (grad * grad)
                root = square * lax.rsqrt(square)
                held[3 * which][some] = (
                    weight[some].astype(jnp.float32)
                    - step_rate * moment * pl.reciprocal(root + adam_epsilon, approx=True)
                ).astype(jnp.bfloat16)
                held[3 * which + 1][some] = moment
                held[3 * which + 2][some] = square
            if (t + 1) * columns % wide == 0:
                for i in range(3 * which, 3 * which + 3):
                    write(t * columns // wide, i).start()

    codes_t = codes_across[...]
    advance(1, codes_t, error_all, decoder)
    signal = inner_last(decoder[...], error_all[...])
    delta_t = jnp.where(codes_t.astype(jnp.float32) > 0, signal, 0.0).astype(jnp.bfloat16)
    advance(0, delta_t, centered, encoder)
    for group in range(groups):
        for i in range(6):
            write(group, i).wait()


def update(total_rows, codes_across, centered, errors, weights, moments):
    latents, width = weights[0].shape
    rows = centered.shape[0]
    columns = next(c for c in (256, 128, width) if width % c == 0)
    full = jax.ShapeDtypeStruct((latents, width), jnp.float32)
    half = jax.ShapeDtypeStruct((latents, width), jnp.bfloat16)
    vmem = pl.BlockSpec(memory_space=pltpu.VMEM)
    wide = pltpu.VMEM((latents, width), jnp.float32)
    narrow = pltpu.VMEM((latents, width), jnp.bfloat16)
    return pl.pallas_call(
        functools.partial(update_kernel, columns, float(total_rows)),
        out_shape=(half, full, full, half, full, full),
        in_specs=[vmem] * (len(errors) + 8),
        out_specs=[pl.BlockSpec(memory_space=pl.ANY)] * 6,
        scratch_shapes=[
            pltpu.VMEM((rows, width), jnp.bfloat16),
            narrow,
            wide,
            wide,
            narrow,
            wide,
            wide,
            pltpu.SemaphoreType.DMA((width // columns, 6)),
        ],
        compiler_params=pltpu.CompilerParams(vmem_limit_bytes=20 * 1024 * 1024 + 8 * rows * width),
        cost_estimate=pl.CostEstimate(
            flops=6 * latents * width * rows,
            bytes_accessed=44 * latents * width,
            transcendentals=4 * latents * width,
        ),
        name="update",
    )(codes_across, centered, *errors, *weights, *moments)


def to_chip(block, distance):
    size = lax.axis_size("latent")
    return lax.ppermute(
        block, "latent", [(i, i ^ (2 * distance)) for i in range(size)]
    )


def to_other_core(block):
    size = lax.axis_size("latent")
    return lax.ppermute(block, "latent", [(i, i ^ 1) for i in range(size)])


def gather_chips(block, chips):
    even = [block] + [to_chip(block, k) for k in range(2, chips, 2)]
    return even, [to_chip(one, 1) for one in even]


def in_turn(even, odd):
    return [one for both in zip(even, odd) for one in both]


def body(
    activations,
    encoder,
    encoder_bias,
    decoder,
    decoder_bias,
    encoder_moment,
    encoder_square,
    decoder_moment,
    decoder_square,
):
    rows_here, width = activations.shape
    latents_here = encoder.shape[0]
    size = lax.axis_size("latent")
    chips = size // 2
    total_rows = rows_here * size

    rows_core = jnp.concatenate(in_turn(*gather_chips(activations, chips)), 0)
    encoder_both = jnp.concatenate([encoder, to_other_core(encoder)], 0)
    decoder_both = jnp.concatenate([decoder, to_other_core(decoder)], 0)
    bias_both = jnp.concatenate([encoder_bias, to_other_core(encoder_bias)], 0)

    centered = (rows_core.astype(jnp.float32) - decoder_bias).astype(jnp.bfloat16)
    codes = jnp.maximum(inner_last(centered, encoder_both) + bias_both, 0.0).astype(
        jnp.bfloat16
    )
    other_codes = to_other_core(codes[:, latents_here:])
    other_centered = to_other_core(centered)

    quad = 4 * rows_here
    parts = []
    for rows in (slice(0, quad), slice(quad, None)):
        sums = jnp.dot(codes[rows], decoder_both, preferred_element_type=jnp.float32)
        parts += [sums[at : at + rows_here] for at in range(0, sums.shape[0], rows_here)]

    def pair_sums(first, last, after=None):
        given = jnp.concatenate(parts[first + 1 : last : 2], 0).astype(jnp.bfloat16)
        if after is not None:
            given, _ = lax.optimization_barrier((given, after))
        came = to_chip(given, 1)
        return [
            parts[k] + came[at * rows_here : (at + 1) * rows_here].astype(jnp.float32)
            for at, k in enumerate(range(first, last, 2))
        ]

    far = [one.astype(jnp.bfloat16) for one in pair_sums(4, chips)]
    own, near = pair_sums(0, 4, (other_codes, other_centered))
    summed = own + to_chip(near.astype(jnp.bfloat16), 2).astype(jnp.float32)
    for k, one in enumerate(far, 2):
        summed = summed + to_chip(one, 2 * k).astype(jnp.float32)
    row_error = (summed - centered[:rows_here].astype(jnp.float32)).astype(jnp.bfloat16)

    row_error, other_codes, other_centered = lax.optimization_barrier(
        (row_error, other_codes, other_centered)
    )
    blocks = in_turn(*gather_chips(row_error, chips))
    errors = [jnp.concatenate(blocks, 0)]
    errors += [to_other_core(jnp.concatenate(one, 0)) for one in (blocks[:4], blocks[4:])]
    codes_across = jnp.concatenate([codes[:, :latents_here], other_codes], 0).T
    centered_all = jnp.concatenate([centered, other_centered], 0)
    (
        encoder_next,
        encoder_moment_next,
        encoder_square_next,
        decoder_next,
        decoder_moment_next,
        decoder_square_next,
    ) = update(
        total_rows,
        codes_across,
        centered_all,
        errors,
        (encoder, decoder),
        (encoder_moment, encoder_square, decoder_moment, decoder_square),
    )
    return (
        row_error,
        encoder_next,
        decoder_next,
        encoder_moment_next,
        encoder_square_next,
        decoder_moment_next,
        decoder_square_next,
    )


def solution(mesh):
    sharded = P(("groups", "latent"), None)
    return jax.shard_map(
        body,
        mesh=mesh,
        in_specs=(
            sharded,
            sharded,
            P(("groups", "latent")),
            sharded,
            P("groups"),
            sharded,
            sharded,
            sharded,
            sharded,
        ),
        out_specs=(sharded,) * 7,
        check_vma=False,
    )
```

```python
import functools

import jax
import jax.numpy as jnp
from jax import lax
from jax.experimental import pallas as pl
from jax.experimental.pallas import tpu as pltpu
from jax.sharding import PartitionSpec as P

beta_first = 0.9
beta_second = 0.999
step_rate = 0.001
adam_epsilon = 1e-08


def inner_last(left, right):
    return lax.dot_general(
        left, right, (((1,), (1,)), ((), ())), preferred_element_type=jnp.float32
    )


def update_kernel(columns, places, rows_total, codes_across, centered, *refs):
    blocks = len(refs) - 20
    errors, (encoder, decoder) = refs[:blocks], refs[blocks : blocks + 2]
    moments = refs[blocks + 2 : blocks + 6]
    outs = refs[blocks + 6 : blocks + 12]
    error_all, *held, sem = refs[blocks + 12 :]
    tiles = encoder.shape[1] // columns
    part = min(32, encoder.shape[0])

    def write(t, i):
        at = pl.ds(t * columns, columns)
        return pltpu.make_async_copy(held[i].at[:, at], outs[i].at[:, at], sem.at[t, i])

    own, *other = errors
    rows = own.shape[0] // len(places)
    for k, place in enumerate(places):
        error_all[pl.ds(place * rows, rows), :] = own[pl.ds(k * rows, rows), :]
    start = own.shape[0]
    for one in other:
        error_all[pl.ds(start, one.shape[0]), :] = one[...]
        start += one.shape[0]
    first = (1.0 - beta_first) / rows_total
    second = (1.0 - beta_second) / (rows_total * rows_total)

    def advance(which, left, right, weight):
        for t in range(tiles):
            at = pl.ds(t * columns, columns)
            total = jnp.dot(left, right[:, at], preferred_element_type=jnp.float32)
            for start in range(0, total.shape[0], part):
                some = (pl.ds(start, part), at)
                grad = total[start : start + part]
                moment = beta_first * moments[2 * which][some] + first * grad
                square = beta_second * moments[2 * which + 1][some] + second * (grad * grad)
                root = square * lax.rsqrt(square)
                held[3 * which][some] = (
                    weight[some].astype(jnp.float32)
                    - step_rate * moment * pl.reciprocal(root + adam_epsilon, approx=True)
                ).astype(jnp.bfloat16)
                held[3 * which + 1][some] = moment
                held[3 * which + 2][some] = square
            for i in range(3 * which, 3 * which + 3):
                write(t, i).start()

    codes_t = codes_across[...]
    advance(1, codes_t, error_all, decoder)
    signal = inner_last(decoder[...], error_all[...])
    delta_t = jnp.where(codes_t.astype(jnp.float32) > 0, signal, 0.0).astype(jnp.bfloat16)
    advance(0, delta_t, centered, encoder)
    for t in range(tiles):
        for i in range(6):
            write(t, i).wait()


def update(total_rows, codes_across, centered, errors, places, weights, moments):
    latents, width = weights[0].shape
    rows = centered.shape[0]
    columns = next(c for c in (256, 128, width) if width % c == 0)
    full = jax.ShapeDtypeStruct((latents, width), jnp.float32)
    half = jax.ShapeDtypeStruct((latents, width), jnp.bfloat16)
    vmem = pl.BlockSpec(memory_space=pltpu.VMEM)
    wide = pltpu.VMEM((latents, width), jnp.float32)
    narrow = pltpu.VMEM((latents, width), jnp.bfloat16)
    return pl.pallas_call(
        functools.partial(update_kernel, columns, places, float(total_rows)),
        out_shape=(half, full, full, half, full, full),
        in_specs=[vmem] * (len(errors) + 8),
        out_specs=[pl.BlockSpec(memory_space=pl.ANY)] * 6,
        scratch_shapes=[
            pltpu.VMEM((rows, width), jnp.bfloat16),
            narrow,
            wide,
            wide,
            narrow,
            wide,
            wide,
            pltpu.SemaphoreType.DMA((width // columns, 6)),
        ],
        compiler_params=pltpu.CompilerParams(vmem_limit_bytes=20 * 1024 * 1024 + 8 * rows * width),
        cost_estimate=pl.CostEstimate(
            flops=6 * latents * width * rows,
            bytes_accessed=44 * latents * width,
            transcendentals=4 * latents * width,
        ),
        name="update",
    )(codes_across, centered, *errors, *weights, *moments)


def to_chip(block, distance):
    size = lax.axis_size("latent")
    return lax.ppermute(
        block, "latent", [(i, i ^ (2 * distance)) for i in range(size)]
    )


def to_other_core(block):
    size = lax.axis_size("latent")
    return lax.ppermute(block, "latent", [(i, i ^ 1) for i in range(size)])


def gather_chips(block, chips):
    even = [block] + [to_chip(block, k) for k in range(2, chips, 2)]
    return even, [to_chip(one, 1) for one in even]


def in_turn(even, odd):
    return [one for both in zip(even, odd) for one in both]


def body(
    activations,
    encoder,
    encoder_bias,
    decoder,
    decoder_bias,
    encoder_moment,
    encoder_square,
    decoder_moment,
    decoder_square,
):
    rows_here, width = activations.shape
    latents_here = encoder.shape[0]
    size = lax.axis_size("latent")
    chips = size // 2
    total_rows = rows_here * size

    rows_core = jnp.concatenate(in_turn(*gather_chips(activations, chips)), 0)
    encoder_both = jnp.concatenate([encoder, to_other_core(encoder)], 0)
    decoder_both = jnp.concatenate([decoder, to_other_core(decoder)], 0)
    bias_both = jnp.concatenate([encoder_bias, to_other_core(encoder_bias)], 0)

    centered = (rows_core.astype(jnp.float32) - decoder_bias).astype(jnp.bfloat16)
    codes = jnp.maximum(inner_last(centered, encoder_both) + bias_both, 0.0).astype(
        jnp.bfloat16
    )
    other_codes = to_other_core(codes[:, latents_here:])

    quad = 4 * rows_here
    parts = []
    for rows in (slice(0, quad), slice(quad, None)):
        sums = jnp.dot(codes[rows], decoder_both, preferred_element_type=jnp.float32)
        parts += [sums[at : at + rows_here] for at in range(0, sums.shape[0], rows_here)]

    def given(first, last):
        return jnp.concatenate(parts[first + 1 : last : 2], 0).astype(jnp.bfloat16)

    def pair_sums(first, last, sent):
        came = to_chip(sent, 1)
        return [
            parts[k] + came[at * rows_here : (at + 1) * rows_here].astype(jnp.float32)
            for at, k in enumerate(range(first, last, 2))
        ]

    far_sent = given(4, chips)
    far = [one.astype(jnp.bfloat16) for one in pair_sums(4, chips, far_sent)]
    later_centered, _ = lax.optimization_barrier((centered, far_sent))
    other_centered = to_other_core(later_centered)
    near_sent, _ = lax.optimization_barrier((given(0, 4), (other_codes, other_centered)))
    own, near = pair_sums(0, 4, near_sent)
    summed = own + to_chip(near.astype(jnp.bfloat16), 2).astype(jnp.float32)
    for k, one in enumerate(far, 2):
        summed = summed + to_chip(one, 2 * k).astype(jnp.float32)
    row_error = (summed - centered[:rows_here].astype(jnp.float32)).astype(jnp.bfloat16)

    row_error, other_codes, other_centered = lax.optimization_barrier(
        (row_error, other_codes, other_centered)
    )
    blocks = in_turn(*gather_chips(row_error, chips))
    places = [0] + list(range(2, chips - 2)) + [1, chips - 2, chips - 1]
    errors = [jnp.concatenate([blocks[k] for k in places], 0)]
    errors += [to_other_core(jnp.concatenate(one, 0)) for one in (blocks[:4], blocks[4:])]
    codes_across = jnp.concatenate([codes[:, :latents_here], other_codes], 0).T
    centered_all = jnp.concatenate([centered, other_centered], 0)
    (
        encoder_next,
        encoder_moment_next,
        encoder_square_next,
        decoder_next,
        decoder_moment_next,
        decoder_square_next,
    ) = update(
        total_rows,
        codes_across,
        centered_all,
        errors,
        places,
        (encoder, decoder),
        (encoder_moment, encoder_square, decoder_moment, decoder_square),
    )
    return (
        row_error,
        encoder_next,
        decoder_next,
        encoder_moment_next,
        encoder_square_next,
        decoder_moment_next,
        decoder_square_next,
    )


def solution(mesh):
    sharded = P(("groups", "latent"), None)
    return jax.shard_map(
        body,
        mesh=mesh,
        in_specs=(
            sharded,
            sharded,
            P(("groups", "latent")),
            sharded,
            P("groups"),
            sharded,
            sharded,
            sharded,
            sharded,
        ),
        out_specs=(sharded,) * 7,
        check_vma=False,
    )
```

```python
import functools

import jax
import jax.numpy as jnp
from jax import lax
from jax.experimental import pallas as pl
from jax.experimental.pallas import tpu as pltpu
from jax.sharding import PartitionSpec as P

beta_first = 0.9
beta_second = 0.999
step_rate = 0.001
adam_epsilon = 1e-08


def inner_last(left, right):
    return lax.dot_general(
        left, right, (((1,), (1,)), ((), ())), preferred_element_type=jnp.float32
    )


def update_kernel(columns, rows_total, codes_across, centered, *refs):
    blocks = len(refs) - 20
    errors, (encoder, decoder) = refs[:blocks], refs[blocks : blocks + 2]
    moments = refs[blocks + 2 : blocks + 6]
    outs = refs[blocks + 6 : blocks + 12]
    error_all, *held, sem = refs[blocks + 12 :]
    tiles = encoder.shape[1] // columns
    part = min(32, encoder.shape[0])

    def write(t, i):
        at = pl.ds(t * columns, columns)
        return pltpu.make_async_copy(held[i].at[:, at], outs[i].at[:, at], sem.at[t, i])

    start = 0
    for one in errors:
        error_all[pl.ds(start, one.shape[0]), :] = one[...]
        start += one.shape[0]
    first = (1.0 - beta_first) / rows_total
    second = (1.0 - beta_second) / (rows_total * rows_total)

    def advance(which, left, right, weight):
        for t in range(tiles):
            at = pl.ds(t * columns, columns)
            total = jnp.dot(left, right[:, at], preferred_element_type=jnp.float32)
            for start in range(0, total.shape[0], part):
                some = (pl.ds(start, part), at)
                grad = total[start : start + part]
                moment = beta_first * moments[2 * which][some] + first * grad
                square = beta_second * moments[2 * which + 1][some] + second * (grad * grad)
                root = square * lax.rsqrt(square)
                held[3 * which][some] = (
                    weight[some].astype(jnp.float32)
                    - step_rate * moment * pl.reciprocal(root + adam_epsilon, approx=True)
                ).astype(jnp.bfloat16)
                held[3 * which + 1][some] = moment
                held[3 * which + 2][some] = square
            for i in range(3 * which, 3 * which + 3):
                write(t, i).start()

    codes_t = codes_across[...]
    advance(1, codes_t, error_all, decoder)
    signal = inner_last(decoder[...], error_all[...])
    delta_t = jnp.where(codes_t.astype(jnp.float32) > 0, signal, 0.0).astype(jnp.bfloat16)
    advance(0, delta_t, centered, encoder)
    for t in range(tiles):
        for i in range(6):
            write(t, i).wait()


def update(total_rows, codes_across, centered, errors, weights, moments):
    latents, width = weights[0].shape
    rows = centered.shape[0]
    columns = next(c for c in (256, 128, width) if width % c == 0)
    full = jax.ShapeDtypeStruct((latents, width), jnp.float32)
    half = jax.ShapeDtypeStruct((latents, width), jnp.bfloat16)
    vmem = pl.BlockSpec(memory_space=pltpu.VMEM)
    wide = pltpu.VMEM((latents, width), jnp.float32)
    narrow = pltpu.VMEM((latents, width), jnp.bfloat16)
    return pl.pallas_call(
        functools.partial(update_kernel, columns, float(total_rows)),
        out_shape=(half, full, full, half, full, full),
        in_specs=[vmem] * (len(errors) + 8),
        out_specs=[pl.BlockSpec(memory_space=pl.ANY)] * 6,
        scratch_shapes=[
            pltpu.VMEM((rows, width), jnp.bfloat16),
            narrow,
            wide,
            wide,
            narrow,
            wide,
            wide,
            pltpu.SemaphoreType.DMA((width // columns, 6)),
        ],
        compiler_params=pltpu.CompilerParams(vmem_limit_bytes=20 * 1024 * 1024 + 8 * rows * width),
        cost_estimate=pl.CostEstimate(
            flops=6 * latents * width * rows,
            bytes_accessed=44 * latents * width,
            transcendentals=4 * latents * width,
        ),
        name="update",
    )(codes_across, centered, *errors, *weights, *moments)


def to_chip(block, distance):
    size = lax.axis_size("latent")
    return lax.ppermute(
        block, "latent", [(i, i ^ (2 * distance)) for i in range(size)]
    )


def to_other_core(block):
    size = lax.axis_size("latent")
    return lax.ppermute(block, "latent", [(i, i ^ 1) for i in range(size)])


def gather_chips(block, chips, after=None):
    later = block
    if after is not None:
        later, _ = lax.optimization_barrier((block, after))
    even = [later] + [to_chip(later, k) for k in range(2, chips, 2)]
    return even, [to_chip(one, 1) for one in even]


def in_turn(even, odd):
    return [one for both in zip(even, odd) for one in both]


def body(
    activations,
    encoder,
    encoder_bias,
    decoder,
    decoder_bias,
    encoder_moment,
    encoder_square,
    decoder_moment,
    decoder_square,
):
    rows_here, width = activations.shape
    latents_here = encoder.shape[0]
    size = lax.axis_size("latent")
    chips = size // 2
    total_rows = rows_here * size

    others = [to_other_core(one) for one in (encoder_bias, encoder, decoder)]
    even, odd = gather_chips(activations, chips, others)
    rows_core = jnp.concatenate(in_turn(even, odd), 0)
    mine, _ = lax.optimization_barrier(((encoder_bias, encoder, decoder), odd[0]))
    bias_both, encoder_both, decoder_both = (
        jnp.concatenate(both, 0) for both in zip(mine, others)
    )

    centered = (rows_core.astype(jnp.float32) - decoder_bias).astype(jnp.bfloat16)
    codes = jnp.maximum(inner_last(centered, encoder_both) + bias_both, 0.0).astype(
        jnp.bfloat16
    )
    other_codes = to_other_core(codes[:, latents_here:])

    quad = 4 * rows_here
    parts = []
    for rows in (slice(0, quad), slice(quad, None)):
        sums = jnp.dot(codes[rows], decoder_both, preferred_element_type=jnp.float32)
        parts += [sums[at : at + rows_here] for at in range(0, sums.shape[0], rows_here)]

    def given(first, last):
        return jnp.concatenate(parts[first + 1 : last : 2], 0).astype(jnp.bfloat16)

    def pair_sums(first, last, sent):
        came = to_chip(sent, 1)
        return [
            parts[k] + came[at * rows_here : (at + 1) * rows_here].astype(jnp.float32)
            for at, k in enumerate(range(first, last, 2))
        ]

    far_sent = given(4, chips)
    far = [one.astype(jnp.bfloat16) for one in pair_sums(4, chips, far_sent)]
    later_centered, _ = lax.optimization_barrier((centered, far_sent))
    other_centered = to_other_core(later_centered)
    near_sent, _ = lax.optimization_barrier((given(0, 4), (other_codes, other_centered)))
    own, near = pair_sums(0, 4, near_sent)
    summed = own + to_chip(near.astype(jnp.bfloat16), 2).astype(jnp.float32)
    for k, one in enumerate(far, 2):
        summed = summed + to_chip(one, 2 * k).astype(jnp.float32)
    row_error = (summed - centered[:rows_here].astype(jnp.float32)).astype(jnp.bfloat16)

    row_error, other_codes, other_centered = lax.optimization_barrier(
        (row_error, other_codes, other_centered)
    )
    blocks = in_turn(*gather_chips(row_error, chips))
    errors = [jnp.concatenate(blocks, 0)]
    errors += [to_other_core(jnp.concatenate(one, 0)) for one in (blocks[:4], blocks[4:])]
    codes_across = jnp.concatenate([codes[:, :latents_here], other_codes], 0).T
    centered_all = jnp.concatenate([centered, other_centered], 0)
    (
        encoder_next,
        encoder_moment_next,
        encoder_square_next,
        decoder_next,
        decoder_moment_next,
        decoder_square_next,
    ) = update(
        total_rows,
        codes_across,
        centered_all,
        errors,
        (encoder, decoder),
        (encoder_moment, encoder_square, decoder_moment, decoder_square),
    )
    return (
        row_error,
        encoder_next,
        decoder_next,
        encoder_moment_next,
        encoder_square_next,
        decoder_moment_next,
        decoder_square_next,
    )


def solution(mesh):
    sharded = P(("groups", "latent"), None)
    return jax.shard_map(
        body,
        mesh=mesh,
        in_specs=(
            sharded,
            sharded,
            P(("groups", "latent")),
            sharded,
            P("groups"),
            sharded,
            sharded,
            sharded,
            sharded,
        ),
        out_specs=(sharded,) * 7,
        check_vma=False,
    )
```

```python
import functools

import jax
import jax.numpy as jnp
from jax import lax
from jax.experimental import pallas as pl
from jax.experimental.pallas import tpu as pltpu
from jax.sharding import PartitionSpec as P

beta_first = 0.9
beta_second = 0.999
step_rate = 0.001
adam_epsilon = 1e-08


def inner_last(left, right):
    return lax.dot_general(
        left, right, (((1,), (1,)), ((), ())), preferred_element_type=jnp.float32
    )


def update_kernel(columns, rows_total, codes_across, centered, *refs):
    blocks = len(refs) - 20
    errors, (encoder, decoder) = refs[:blocks], refs[blocks : blocks + 2]
    moments = refs[blocks + 2 : blocks + 6]
    outs = refs[blocks + 6 : blocks + 12]
    error_all, *held, sem = refs[blocks + 12 :]
    tiles = encoder.shape[1] // columns
    part = min(32, encoder.shape[0])

    def write(t, i):
        at = pl.ds(t * columns, columns)
        return pltpu.make_async_copy(held[i].at[:, at], outs[i].at[:, at], sem.at[t, i])

    start = 0
    for one in errors:
        error_all[pl.ds(start, one.shape[0]), :] = one[...]
        start += one.shape[0]
    first = (1.0 - beta_first) / rows_total
    second = (1.0 - beta_second) / (rows_total * rows_total)

    def advance(which, left, right, weight):
        for t in range(tiles):
            at = pl.ds(t * columns, columns)
            total = jnp.dot(left, right[:, at], preferred_element_type=jnp.float32)
            for start in range(0, total.shape[0], part):
                some = (pl.ds(start, part), at)
                grad = total[start : start + part]
                moment = beta_first * moments[2 * which][some] + first * grad
                square = beta_second * moments[2 * which + 1][some] + second * (grad * grad)
                root = square * lax.rsqrt(square)
                held[3 * which][some] = (
                    weight[some].astype(jnp.float32)
                    - step_rate * moment * pl.reciprocal(root + adam_epsilon, approx=True)
                ).astype(jnp.bfloat16)
                held[3 * which + 1][some] = moment
                held[3 * which + 2][some] = square
            for i in range(3 * which, 3 * which + 3):
                write(t, i).start()

    codes_t = codes_across[...]
    advance(1, codes_t, error_all, decoder)
    signal = inner_last(decoder[...], error_all[...])
    delta_t = jnp.where(codes_t.astype(jnp.float32) > 0, signal, 0.0).astype(jnp.bfloat16)
    advance(0, delta_t, centered, encoder)
    for t in range(tiles):
        for i in range(6):
            write(t, i).wait()


def update(total_rows, codes_across, centered, errors, weights, moments):
    latents, width = weights[0].shape
    rows = centered.shape[0]
    columns = next(c for c in (256, 128, width) if width % c == 0)
    full = jax.ShapeDtypeStruct((latents, width), jnp.float32)
    half = jax.ShapeDtypeStruct((latents, width), jnp.bfloat16)
    vmem = pl.BlockSpec(memory_space=pltpu.VMEM)
    wide = pltpu.VMEM((latents, width), jnp.float32)
    narrow = pltpu.VMEM((latents, width), jnp.bfloat16)
    return pl.pallas_call(
        functools.partial(update_kernel, columns, float(total_rows)),
        out_shape=(half, full, full, half, full, full),
        in_specs=[vmem] * (len(errors) + 8),
        out_specs=[pl.BlockSpec(memory_space=pl.ANY)] * 6,
        scratch_shapes=[
            pltpu.VMEM((rows, width), jnp.bfloat16),
            narrow,
            wide,
            wide,
            narrow,
            wide,
            wide,
            pltpu.SemaphoreType.DMA((width // columns, 6)),
        ],
        compiler_params=pltpu.CompilerParams(vmem_limit_bytes=20 * 1024 * 1024 + 8 * rows * width),
        cost_estimate=pl.CostEstimate(
            flops=6 * latents * width * rows,
            bytes_accessed=44 * latents * width,
            transcendentals=4 * latents * width,
        ),
        name="update",
    )(codes_across, centered, *errors, *weights, *moments)


def to_chip(block, distance):
    size = lax.axis_size("latent")
    return lax.ppermute(
        block, "latent", [(i, i ^ (2 * distance)) for i in range(size)]
    )


def to_other_core(block):
    size = lax.axis_size("latent")
    return lax.ppermute(block, "latent", [(i, i ^ 1) for i in range(size)])


def gather_chips(block, chips):
    even = [block] + [to_chip(block, k) for k in range(2, chips, 2)]
    return even, [to_chip(one, 1) for one in even]


def in_turn(even, odd):
    return [one for both in zip(even, odd) for one in both]


def body(
    activations,
    encoder,
    encoder_bias,
    decoder,
    decoder_bias,
    encoder_moment,
    encoder_square,
    decoder_moment,
    decoder_square,
):
    rows_here, width = activations.shape
    latents_here = encoder.shape[0]
    size = lax.axis_size("latent")
    chips = size // 2
    total_rows = rows_here * size

    rows_core = jnp.concatenate(in_turn(*gather_chips(activations, chips)), 0)
    encoder_both = jnp.concatenate([encoder, to_other_core(encoder)], 0)
    decoder_both = jnp.concatenate([decoder, to_other_core(decoder)], 0)
    bias_both = jnp.concatenate([encoder_bias, to_other_core(encoder_bias)], 0)

    centered = (rows_core.astype(jnp.float32) - decoder_bias).astype(jnp.bfloat16)
    codes = jnp.maximum(inner_last(centered, encoder_both) + bias_both, 0.0).astype(
        jnp.bfloat16
    )
    other_codes = to_other_core(codes[:, latents_here:])

    quad = 4 * rows_here
    parts = []
    for rows in (slice(0, quad), slice(quad, None)):
        sums = jnp.dot(codes[rows], decoder_both, preferred_element_type=jnp.float32)
        parts += [sums[at : at + rows_here] for at in range(0, sums.shape[0], rows_here)]

    def given(first, last):
        return jnp.concatenate(parts[first + 1 : last : 2], 0).astype(jnp.bfloat16)

    def pair_sums(first, last, sent):
        came = to_chip(sent, 1)
        return [
            parts[k] + came[at * rows_here : (at + 1) * rows_here].astype(jnp.float32)
            for at, k in enumerate(range(first, last, 2))
        ]

    far_sent = given(4, chips)
    far = [one.astype(jnp.bfloat16) for one in pair_sums(4, chips, far_sent)]
    later_centered, _ = lax.optimization_barrier((centered, far_sent))
    other_centered = to_other_core(later_centered)
    near_sent, _ = lax.optimization_barrier((given(0, 4), (other_codes, other_centered)))
    own, near = pair_sums(0, 4, near_sent)
    summed = own + to_chip(near.astype(jnp.bfloat16), 2).astype(jnp.float32)
    for k, one in enumerate(far, 2):
        summed = summed + to_chip(one, 2 * k).astype(jnp.float32)
    row_error = (summed - centered[:rows_here].astype(jnp.float32)).astype(jnp.bfloat16)

    row_error, other_codes, other_centered = lax.optimization_barrier(
        (row_error, other_codes, other_centered)
    )
    blocks = in_turn(*gather_chips(row_error, chips))
    errors = [jnp.concatenate(blocks, 0)]
    errors += [to_other_core(jnp.concatenate(one, 0)) for one in (blocks[:4], blocks[4:])]
    codes_across = jnp.concatenate([codes[:, :latents_here], other_codes], 0).T
    centered_all = jnp.concatenate([centered, other_centered], 0)
    (
        encoder_next,
        encoder_moment_next,
        encoder_square_next,
        decoder_next,
        decoder_moment_next,
        decoder_square_next,
    ) = update(
        total_rows,
        codes_across,
        centered_all,
        errors,
        (encoder, decoder),
        (encoder_moment, encoder_square, decoder_moment, decoder_square),
    )
    return (
        row_error,
        encoder_next,
        decoder_next,
        encoder_moment_next,
        encoder_square_next,
        decoder_moment_next,
        decoder_square_next,
    )


def solution(mesh):
    sharded = P(("groups", "latent"), None)
    return jax.shard_map(
        body,
        mesh=mesh,
        in_specs=(
            sharded,
            sharded,
            P(("groups", "latent")),
            sharded,
            P("groups"),
            sharded,
            sharded,
            sharded,
            sharded,
        ),
        out_specs=(sharded,) * 7,
        check_vma=False,
    )
```

```python
import functools

import jax
import jax.numpy as jnp
from jax import lax
from jax.experimental import pallas as pl
from jax.experimental.pallas import tpu as pltpu
from jax.sharding import PartitionSpec as P

beta_first = 0.9
beta_second = 0.999
step_rate = 0.001
adam_epsilon = 1e-08


def inner_last(left, right):
    return lax.dot_general(
        left, right, (((1,), (1,)), ((), ())), preferred_element_type=jnp.float32
    )


def own_kernel(columns, codes_across, centered, errors, decoder, encoder_total, decoder_total):
    codes_t = codes_across[...]
    signal = inner_last(decoder[...], errors[...])
    delta_t = jnp.where(codes_t.astype(jnp.float32) > 0, signal, 0.0).astype(jnp.bfloat16)
    for start in range(0, decoder.shape[1], columns):
        at = pl.ds(start, columns)
        decoder_total[:, at] = jnp.dot(
            codes_t, errors[:, at], preferred_element_type=jnp.float32
        )
        encoder_total[:, at] = jnp.dot(
            delta_t, centered[:, at], preferred_element_type=jnp.float32
        )


def own_totals(codes_across, centered, errors, decoder):
    latents, width = decoder.shape
    rows = centered.shape[0]
    vmem = pl.BlockSpec(memory_space=pltpu.VMEM)
    total = jax.ShapeDtypeStruct((latents, width), jnp.float32)
    return pl.pallas_call(
        functools.partial(own_kernel, columns_of(width)),
        out_shape=(total, total),
        in_specs=[vmem] * 4,
        out_specs=[vmem] * 2,
        compiler_params=pltpu.CompilerParams(vmem_limit_bytes=16 * 1024 * 1024 + 8 * rows * width),
        cost_estimate=pl.CostEstimate(
            flops=6 * latents * width * rows,
            bytes_accessed=12 * latents * width + 4 * rows * width,
            transcendentals=0,
        ),
        name="own_totals",
    )(codes_across, centered, errors, decoder)


def columns_of(width):
    return next(c for c in (256, 128, width) if width % c == 0)


def update_kernel(columns, rows_total, codes_across, centered, *refs):
    blocks = len(refs) - 22
    errors, (encoder, decoder) = refs[:blocks], refs[blocks : blocks + 2]
    moments = refs[blocks + 2 : blocks + 6]
    totals = refs[blocks + 6 : blocks + 8]
    outs = refs[blocks + 8 : blocks + 14]
    error_all, *held, sem = refs[blocks + 14 :]
    tiles = encoder.shape[1] // columns
    part = min(32, encoder.shape[0])

    def write(t, i):
        at = pl.ds(t * columns, columns)
        return pltpu.make_async_copy(held[i].at[:, at], outs[i].at[:, at], sem.at[t, i])

    start = 0
    for one in errors:
        error_all[pl.ds(start, one.shape[0]), :] = one[...]
        start += one.shape[0]
    first = (1.0 - beta_first) / rows_total
    second = (1.0 - beta_second) / (rows_total * rows_total)

    def advance(which, left, right, weight):
        for t in range(tiles):
            at = pl.ds(t * columns, columns)
            total = jnp.dot(left, right[:, at], preferred_element_type=jnp.float32)
            for start in range(0, total.shape[0], part):
                some = (pl.ds(start, part), at)
                grad = totals[which][some] + total[start : start + part]
                moment = beta_first * moments[2 * which][some] + first * grad
                square = beta_second * moments[2 * which + 1][some] + second * (grad * grad)
                root = square * lax.rsqrt(square)
                held[3 * which][some] = (
                    weight[some].astype(jnp.float32)
                    - step_rate * moment * pl.reciprocal(root + adam_epsilon, approx=True)
                ).astype(jnp.bfloat16)
                held[3 * which + 1][some] = moment
                held[3 * which + 2][some] = square
            for i in range(3 * which, 3 * which + 3):
                write(t, i).start()

    codes_t = codes_across[...]
    advance(1, codes_t, error_all, decoder)
    signal = inner_last(decoder[...], error_all[...])
    delta_t = jnp.where(codes_t.astype(jnp.float32) > 0, signal, 0.0).astype(jnp.bfloat16)
    advance(0, delta_t, centered, encoder)
    for t in range(tiles):
        for i in range(6):
            write(t, i).wait()


def update(total_rows, codes_across, centered, errors, weights, moments, totals):
    latents, width = weights[0].shape
    rows = centered.shape[0]
    columns = columns_of(width)
    full = jax.ShapeDtypeStruct((latents, width), jnp.float32)
    half = jax.ShapeDtypeStruct((latents, width), jnp.bfloat16)
    vmem = pl.BlockSpec(memory_space=pltpu.VMEM)
    wide = pltpu.VMEM((latents, width), jnp.float32)
    narrow = pltpu.VMEM((latents, width), jnp.bfloat16)
    return pl.pallas_call(
        functools.partial(update_kernel, columns, float(total_rows)),
        out_shape=(half, full, full, half, full, full),
        in_specs=[vmem] * (len(errors) + 10),
        out_specs=[pl.BlockSpec(memory_space=pl.ANY)] * 6,
        scratch_shapes=[
            pltpu.VMEM((rows, width), jnp.bfloat16),
            narrow,
            wide,
            wide,
            narrow,
            wide,
            wide,
            pltpu.SemaphoreType.DMA((width // columns, 6)),
        ],
        compiler_params=pltpu.CompilerParams(vmem_limit_bytes=20 * 1024 * 1024 + 8 * rows * width),
        cost_estimate=pl.CostEstimate(
            flops=6 * latents * width * rows,
            bytes_accessed=44 * latents * width,
            transcendentals=4 * latents * width,
        ),
        name="update",
    )(codes_across, centered, *errors, *weights, *moments, *totals)


def to_chip(block, distance):
    size = lax.axis_size("latent")
    return lax.ppermute(
        block, "latent", [(i, i ^ (2 * distance)) for i in range(size)]
    )


def to_other_core(block):
    size = lax.axis_size("latent")
    return lax.ppermute(block, "latent", [(i, i ^ 1) for i in range(size)])


def gather_chips(block, chips):
    even = [block] + [to_chip(block, k) for k in range(2, chips, 2)]
    return even, [to_chip(one, 1) for one in even]


def in_turn(even, odd):
    return [one for both in zip(even, odd) for one in both]


def body(
    activations,
    encoder,
    encoder_bias,
    decoder,
    decoder_bias,
    encoder_moment,
    encoder_square,
    decoder_moment,
    decoder_square,
):
    rows_here, width = activations.shape
    latents_here = encoder.shape[0]
    size = lax.axis_size("latent")
    chips = size // 2
    total_rows = rows_here * size

    rows_core = jnp.concatenate(in_turn(*gather_chips(activations, chips)), 0)
    encoder_both = jnp.concatenate([encoder, to_other_core(encoder)], 0)
    decoder_both = jnp.concatenate([decoder, to_other_core(decoder)], 0)
    bias_both = jnp.concatenate([encoder_bias, to_other_core(encoder_bias)], 0)

    centered = (rows_core.astype(jnp.float32) - decoder_bias).astype(jnp.bfloat16)
    codes = jnp.maximum(inner_last(centered, encoder_both) + bias_both, 0.0).astype(
        jnp.bfloat16
    )
    other_codes = to_other_core(codes[:, latents_here:])

    quad = 4 * rows_here
    parts = []
    for rows in (slice(0, quad), slice(quad, None)):
        sums = jnp.dot(codes[rows], decoder_both, preferred_element_type=jnp.float32)
        parts += [sums[at : at + rows_here] for at in range(0, sums.shape[0], rows_here)]

    def given(first, last):
        return jnp.concatenate(parts[first + 1 : last : 2], 0).astype(jnp.bfloat16)

    def pair_sums(first, last, sent):
        came = to_chip(sent, 1)
        return [
            parts[k] + came[at * rows_here : (at + 1) * rows_here].astype(jnp.float32)
            for at, k in enumerate(range(first, last, 2))
        ]

    far_sent = given(4, chips)
    far = [one.astype(jnp.bfloat16) for one in pair_sums(4, chips, far_sent)]
    later_centered, _ = lax.optimization_barrier((centered, far_sent))
    other_centered = to_other_core(later_centered)
    near_sent, _ = lax.optimization_barrier((given(0, 4), (other_codes, other_centered)))
    own, near = pair_sums(0, 4, near_sent)
    summed = own + to_chip(near.astype(jnp.bfloat16), 2).astype(jnp.float32)
    for k, one in enumerate(far, 2):
        summed = summed + to_chip(one, 2 * k).astype(jnp.float32)
    row_error = (summed - centered[:rows_here].astype(jnp.float32)).astype(jnp.bfloat16)

    row_error, other_codes, other_centered = lax.optimization_barrier(
        (row_error, other_codes, other_centered)
    )
    blocks = in_turn(*gather_chips(row_error, chips))
    errors = jnp.concatenate(blocks, 0)
    other_errors = [to_other_core(jnp.concatenate(one, 0)) for one in (blocks[:4], blocks[4:])]
    totals = own_totals(codes[:, :latents_here].T, centered, errors, decoder)
    (
        encoder_next,
        encoder_moment_next,
        encoder_square_next,
        decoder_next,
        decoder_moment_next,
        decoder_square_next,
    ) = update(
        total_rows,
        other_codes.T,
        other_centered,
        other_errors,
        (encoder, decoder),
        (encoder_moment, encoder_square, decoder_moment, decoder_square),
        totals,
    )
    return (
        row_error,
        encoder_next,
        decoder_next,
        encoder_moment_next,
        encoder_square_next,
        decoder_moment_next,
        decoder_square_next,
    )


def solution(mesh):
    sharded = P(("groups", "latent"), None)
    return jax.shard_map(
        body,
        mesh=mesh,
        in_specs=(
            sharded,
            sharded,
            P(("groups", "latent")),
            sharded,
            P("groups"),
            sharded,
            sharded,
            sharded,
            sharded,
        ),
        out_specs=(sharded,) * 7,
        check_vma=False,
    )
```

```python
import functools

import jax
import jax.numpy as jnp
from jax import lax
from jax.experimental import pallas as pl
from jax.experimental.pallas import tpu as pltpu
from jax.sharding import PartitionSpec as P

beta_first = 0.9
beta_second = 0.999
step_rate = 0.001
adam_epsilon = 1e-08


def inner_last(left, right):
    return lax.dot_general(
        left, right, (((1,), (1,)), ((), ())), preferred_element_type=jnp.float32
    )


def own_kernel(columns, codes_across, centered, errors, decoder, encoder_total, decoder_total):
    codes_t = codes_across[...]
    signal = inner_last(decoder[...], errors[...])
    delta_t = jnp.where(codes_t.astype(jnp.float32) > 0, signal, 0.0).astype(jnp.bfloat16)
    for start in range(0, decoder.shape[1], columns):
        at = pl.ds(start, columns)
        decoder_total[:, at] = jnp.dot(
            codes_t, errors[:, at], preferred_element_type=jnp.float32
        )
        encoder_total[:, at] = jnp.dot(
            delta_t, centered[:, at], preferred_element_type=jnp.float32
        )


def own_totals(codes_across, centered, errors, decoder):
    latents, width = decoder.shape
    rows = centered.shape[0]
    vmem = pl.BlockSpec(memory_space=pltpu.VMEM)
    total = jax.ShapeDtypeStruct((latents, width), jnp.float32)
    return pl.pallas_call(
        functools.partial(own_kernel, columns_of(width)),
        out_shape=(total, total),
        in_specs=[vmem] * 4,
        out_specs=[vmem] * 2,
        compiler_params=pltpu.CompilerParams(vmem_limit_bytes=16 * 1024 * 1024 + 8 * rows * width),
        cost_estimate=pl.CostEstimate(
            flops=6 * latents * width * rows,
            bytes_accessed=12 * latents * width + 4 * rows * width,
            transcendentals=0,
        ),
        name="own_totals",
    )(codes_across, centered, errors, decoder)


def columns_of(width):
    return next(c for c in (256, 128, width) if width % c == 0)


def update_kernel(columns, rows_total, codes_across, centered, *refs):
    blocks = len(refs) - 22
    errors, (encoder, decoder) = refs[:blocks], refs[blocks : blocks + 2]
    moments = refs[blocks + 2 : blocks + 6]
    totals = refs[blocks + 6 : blocks + 8]
    outs = refs[blocks + 8 : blocks + 14]
    error_all, *held, sem = refs[blocks + 14 :]
    tiles = encoder.shape[1] // columns
    part = min(32, encoder.shape[0])

    def write(t, i):
        at = pl.ds(t * columns, columns)
        return pltpu.make_async_copy(held[i].at[:, at], outs[i].at[:, at], sem.at[t, i])

    start = 0
    for one in errors:
        error_all[pl.ds(start, one.shape[0]), :] = one[...]
        start += one.shape[0]
    first = (1.0 - beta_first) / rows_total
    second = (1.0 - beta_second) / (rows_total * rows_total)

    def advance(which, left, right, weight):
        for t in range(tiles):
            at = pl.ds(t * columns, columns)
            total = jnp.dot(left, right[:, at], preferred_element_type=jnp.float32)
            for start in range(0, total.shape[0], part):
                some = (pl.ds(start, part), at)
                grad = totals[which][some] + total[start : start + part]
                moment = beta_first * moments[2 * which][some] + first * grad
                square = beta_second * moments[2 * which + 1][some] + second * (grad * grad)
                guess = lax.rsqrt(square)
                root = square * guess
                inverse = guess * (2.0 - (root + adam_epsilon) * guess)
                held[3 * which][some] = (
                    weight[some].astype(jnp.float32) - step_rate * moment * inverse
                ).astype(jnp.bfloat16)
                held[3 * which + 1][some] = moment
                held[3 * which + 2][some] = square
            for i in range(3 * which, 3 * which + 3):
                write(t, i).start()

    codes_t = codes_across[...]
    advance(1, codes_t, error_all, decoder)
    signal = inner_last(decoder[...], error_all[...])
    delta_t = jnp.where(codes_t.astype(jnp.float32) > 0, signal, 0.0).astype(jnp.bfloat16)
    advance(0, delta_t, centered, encoder)
    for t in range(tiles):
        for i in range(6):
            write(t, i).wait()


def update(total_rows, codes_across, centered, errors, weights, moments, totals):
    latents, width = weights[0].shape
    rows = centered.shape[0]
    columns = columns_of(width)
    full = jax.ShapeDtypeStruct((latents, width), jnp.float32)
    half = jax.ShapeDtypeStruct((latents, width), jnp.bfloat16)
    vmem = pl.BlockSpec(memory_space=pltpu.VMEM)
    wide = pltpu.VMEM((latents, width), jnp.float32)
    narrow = pltpu.VMEM((latents, width), jnp.bfloat16)
    return pl.pallas_call(
        functools.partial(update_kernel, columns, float(total_rows)),
        out_shape=(half, full, full, half, full, full),
        in_specs=[vmem] * (len(errors) + 10),
        out_specs=[pl.BlockSpec(memory_space=pl.ANY)] * 6,
        scratch_shapes=[
            pltpu.VMEM((rows, width), jnp.bfloat16),
            narrow,
            wide,
            wide,
            narrow,
            wide,
            wide,
            pltpu.SemaphoreType.DMA((width // columns, 6)),
        ],
        compiler_params=pltpu.CompilerParams(vmem_limit_bytes=20 * 1024 * 1024 + 8 * rows * width),
        cost_estimate=pl.CostEstimate(
            flops=6 * latents * width * rows,
            bytes_accessed=44 * latents * width,
            transcendentals=4 * latents * width,
        ),
        name="update",
    )(codes_across, centered, *errors, *weights, *moments, *totals)


def to_chip(block, distance):
    size = lax.axis_size("latent")
    return lax.ppermute(
        block, "latent", [(i, i ^ (2 * distance)) for i in range(size)]
    )


def to_other_core(block):
    size = lax.axis_size("latent")
    return lax.ppermute(block, "latent", [(i, i ^ 1) for i in range(size)])


def gather_chips(block, chips):
    even = [block] + [to_chip(block, k) for k in range(2, chips, 2)]
    return even, [to_chip(one, 1) for one in even]


def in_turn(even, odd):
    return [one for both in zip(even, odd) for one in both]


def body(
    activations,
    encoder,
    encoder_bias,
    decoder,
    decoder_bias,
    encoder_moment,
    encoder_square,
    decoder_moment,
    decoder_square,
):
    rows_here, width = activations.shape
    latents_here = encoder.shape[0]
    size = lax.axis_size("latent")
    chips = size // 2
    total_rows = rows_here * size

    rows_core = jnp.concatenate(in_turn(*gather_chips(activations, chips)), 0)
    encoder_both = jnp.concatenate([encoder, to_other_core(encoder)], 0)
    decoder_both = jnp.concatenate([decoder, to_other_core(decoder)], 0)
    bias_both = jnp.concatenate([encoder_bias, to_other_core(encoder_bias)], 0)

    centered = (rows_core.astype(jnp.float32) - decoder_bias).astype(jnp.bfloat16)
    codes = jnp.maximum(inner_last(centered, encoder_both) + bias_both, 0.0).astype(
        jnp.bfloat16
    )
    other_codes = to_other_core(codes[:, latents_here:])

    quad = 4 * rows_here

    def partial_sums(some_codes):
        sums = jnp.dot(some_codes, decoder_both, preferred_element_type=jnp.float32)
        parts = [sums[at : at + rows_here] for at in range(0, sums.shape[0], rows_here)]
        return parts, jnp.concatenate(parts[1::2], 0).astype(jnp.bfloat16)

    def pair_sums(parts, sent):
        came = to_chip(sent, 1)
        return [
            part + came[at * rows_here : (at + 1) * rows_here].astype(jnp.float32)
            for at, part in enumerate(parts[::2])
        ]

    far_parts, far_sent = partial_sums(codes[quad:])
    far = [one.astype(jnp.bfloat16) for one in pair_sums(far_parts, far_sent)]
    later_centered, _ = lax.optimization_barrier((centered, far_sent))
    other_centered = to_other_core(later_centered)
    near_codes, _ = lax.optimization_barrier((codes[:quad], other_codes))
    near_parts, near_sent = partial_sums(near_codes)
    near_sent, _ = lax.optimization_barrier((near_sent, other_centered))
    own, near = pair_sums(near_parts, near_sent)
    summed = own + to_chip(near.astype(jnp.bfloat16), 2).astype(jnp.float32)
    for k, one in enumerate(far, 2):
        summed = summed + to_chip(one, 2 * k).astype(jnp.float32)
    row_error = (summed - centered[:rows_here].astype(jnp.float32)).astype(jnp.bfloat16)

    row_error, other_codes, other_centered = lax.optimization_barrier(
        (row_error, other_codes, other_centered)
    )
    blocks = in_turn(*gather_chips(row_error, chips))
    errors = jnp.concatenate(blocks, 0)
    other_errors = [to_other_core(jnp.concatenate(one, 0)) for one in (blocks[:4], blocks[4:])]
    totals = own_totals(codes[:, :latents_here].T, centered, errors, decoder)
    (
        encoder_next,
        encoder_moment_next,
        encoder_square_next,
        decoder_next,
        decoder_moment_next,
        decoder_square_next,
    ) = update(
        total_rows,
        other_codes.T,
        other_centered,
        other_errors,
        (encoder, decoder),
        (encoder_moment, encoder_square, decoder_moment, decoder_square),
        totals,
    )
    return (
        row_error,
        encoder_next,
        decoder_next,
        encoder_moment_next,
        encoder_square_next,
        decoder_moment_next,
        decoder_square_next,
    )


def solution(mesh):
    sharded = P(("groups", "latent"), None)
    return jax.shard_map(
        body,
        mesh=mesh,
        in_specs=(
            sharded,
            sharded,
            P(("groups", "latent")),
            sharded,
            P("groups"),
            sharded,
            sharded,
            sharded,
            sharded,
        ),
        out_specs=(sharded,) * 7,
        check_vma=False,
    )
```

```python
import functools

import jax
import jax.numpy as jnp
from jax import lax
from jax.experimental import pallas as pl
from jax.experimental.pallas import tpu as pltpu
from jax.sharding import PartitionSpec as P

beta_first = 0.9
beta_second = 0.999
step_rate = 0.001
adam_epsilon = 1e-08


def inner_last(left, right):
    return lax.dot_general(
        left, right, (((1,), (1,)), ((), ())), preferred_element_type=jnp.float32
    )


def own_kernel(columns, codes_across, centered, errors, decoder, encoder_total, decoder_total):
    codes_t = codes_across[...]
    signal = inner_last(decoder[...], errors[...])
    delta_t = jnp.where(codes_t.astype(jnp.float32) > 0, signal, 0.0).astype(jnp.bfloat16)
    for start in range(0, decoder.shape[1], columns):
        at = pl.ds(start, columns)
        decoder_total[:, at] = jnp.dot(
            codes_t, errors[:, at], preferred_element_type=jnp.float32
        )
        encoder_total[:, at] = jnp.dot(
            delta_t, centered[:, at], preferred_element_type=jnp.float32
        )


def own_totals(codes_across, centered, errors, decoder):
    latents, width = decoder.shape
    rows = centered.shape[0]
    vmem = pl.BlockSpec(memory_space=pltpu.VMEM)
    total = jax.ShapeDtypeStruct((latents, width), jnp.float32)
    return pl.pallas_call(
        functools.partial(own_kernel, columns_of(width)),
        out_shape=(total, total),
        in_specs=[vmem] * 4,
        out_specs=[vmem] * 2,
        compiler_params=pltpu.CompilerParams(vmem_limit_bytes=16 * 1024 * 1024 + 8 * rows * width),
        cost_estimate=pl.CostEstimate(
            flops=6 * latents * width * rows,
            bytes_accessed=12 * latents * width + 4 * rows * width,
            transcendentals=0,
        ),
        name="own_totals",
    )(codes_across, centered, errors, decoder)


def columns_of(width):
    return next(c for c in (256, 128, width) if width % c == 0)


def update_kernel(columns, rows_total, codes_across, centered, *refs):
    blocks = len(refs) - 22
    errors, (encoder, decoder) = refs[:blocks], refs[blocks : blocks + 2]
    moments = refs[blocks + 2 : blocks + 6]
    totals = refs[blocks + 6 : blocks + 8]
    outs = refs[blocks + 8 : blocks + 14]
    error_all, *held, sem = refs[blocks + 14 :]
    tiles = encoder.shape[1] // columns
    part = min(32, encoder.shape[0])

    def write(t, i):
        at = pl.ds(t * columns, columns)
        return pltpu.make_async_copy(held[i].at[:, at], outs[i].at[:, at], sem.at[t, i])

    start = 0
    for one in errors:
        error_all[pl.ds(start, one.shape[0]), :] = one[...]
        start += one.shape[0]
    first = (1.0 - beta_first) / rows_total
    second = (1.0 - beta_second) / (rows_total * rows_total)

    def advance(which, left, right, weight):
        for t in range(tiles):
            at = pl.ds(t * columns, columns)
            total = jnp.dot(left, right[:, at], preferred_element_type=jnp.float32)
            for start in range(0, total.shape[0], part):
                some = (pl.ds(start, part), at)
                grad = totals[which][some] + total[start : start + part]
                moment = beta_first * moments[2 * which][some] + first * grad
                square = beta_second * moments[2 * which + 1][some] + second * (grad * grad)
                root = square * lax.rsqrt(square)
                held[3 * which][some] = (
                    weight[some].astype(jnp.float32)
                    - step_rate * moment * pl.reciprocal(root + adam_epsilon, approx=True)
                ).astype(jnp.bfloat16)
                held[3 * which + 1][some] = moment
                held[3 * which + 2][some] = square
            for i in range(3 * which, 3 * which + 3):
                write(t, i).start()

    codes_t = codes_across[...]
    advance(1, codes_t, error_all, decoder)
    signal = inner_last(decoder[...], error_all[...])
    delta_t = jnp.where(codes_t.astype(jnp.float32) > 0, signal, 0.0).astype(jnp.bfloat16)
    advance(0, delta_t, centered, encoder)
    for t in range(tiles):
        for i in range(6):
            write(t, i).wait()


def update(total_rows, codes_across, centered, errors, weights, moments, totals):
    latents, width = weights[0].shape
    rows = centered.shape[0]
    columns = columns_of(width)
    full = jax.ShapeDtypeStruct((latents, width), jnp.float32)
    half = jax.ShapeDtypeStruct((latents, width), jnp.bfloat16)
    vmem = pl.BlockSpec(memory_space=pltpu.VMEM)
    wide = pltpu.VMEM((latents, width), jnp.float32)
    narrow = pltpu.VMEM((latents, width), jnp.bfloat16)
    return pl.pallas_call(
        functools.partial(update_kernel, columns, float(total_rows)),
        out_shape=(half, full, full, half, full, full),
        in_specs=[vmem] * (len(errors) + 10),
        out_specs=[pl.BlockSpec(memory_space=pl.ANY)] * 6,
        scratch_shapes=[
            pltpu.VMEM((rows, width), jnp.bfloat16),
            narrow,
            wide,
            wide,
            narrow,
            wide,
            wide,
            pltpu.SemaphoreType.DMA((width // columns, 6)),
        ],
        compiler_params=pltpu.CompilerParams(vmem_limit_bytes=20 * 1024 * 1024 + 8 * rows * width),
        cost_estimate=pl.CostEstimate(
            flops=6 * latents * width * rows,
            bytes_accessed=44 * latents * width,
            transcendentals=4 * latents * width,
        ),
        name="update",
    )(codes_across, centered, *errors, *weights, *moments, *totals)


def to_chip(block, distance):
    size = lax.axis_size("latent")
    return lax.ppermute(
        block, "latent", [(i, i ^ (2 * distance)) for i in range(size)]
    )


def to_other_core(block):
    size = lax.axis_size("latent")
    return lax.ppermute(block, "latent", [(i, i ^ 1) for i in range(size)])


def gather_chips(block, chips):
    even = [block] + [to_chip(block, k) for k in range(2, chips, 2)]
    return even, [to_chip(one, 1) for one in even]


def in_turn(even, odd):
    return [one for both in zip(even, odd) for one in both]


def body(
    activations,
    encoder,
    encoder_bias,
    decoder,
    decoder_bias,
    encoder_moment,
    encoder_square,
    decoder_moment,
    decoder_square,
):
    rows_here, width = activations.shape
    latents_here = encoder.shape[0]
    size = lax.axis_size("latent")
    chips = size // 2
    total_rows = rows_here * size

    rows_core = jnp.concatenate(in_turn(*gather_chips(activations, chips)), 0)
    encoder_both = jnp.concatenate([encoder, to_other_core(encoder)], 0)
    decoder_both = jnp.concatenate([decoder, to_other_core(decoder)], 0)
    bias_both = jnp.concatenate([encoder_bias, to_other_core(encoder_bias)], 0)

    centered = (rows_core.astype(jnp.float32) - decoder_bias).astype(jnp.bfloat16)
    codes = jnp.maximum(inner_last(centered, encoder_both) + bias_both, 0.0).astype(
        jnp.bfloat16
    )
    other_codes = to_other_core(codes[:, latents_here:])

    quad = 4 * rows_here

    def partial_sums(some_codes):
        sums = jnp.dot(some_codes, decoder_both, preferred_element_type=jnp.float32)
        parts = [sums[at : at + rows_here] for at in range(0, sums.shape[0], rows_here)]
        return parts, jnp.concatenate(parts[1::2], 0).astype(jnp.bfloat16)

    def pair_sums(parts, sent):
        came = to_chip(sent, 1)
        return [
            part + came[at * rows_here : (at + 1) * rows_here].astype(jnp.float32)
            for at, part in enumerate(parts[::2])
        ]

    far_parts, far_sent = partial_sums(codes[quad:])
    far = [one.astype(jnp.bfloat16) for one in pair_sums(far_parts, far_sent)]
    later_centered, _ = lax.optimization_barrier((centered, far_sent))
    other_centered = to_other_core(later_centered)
    near_codes, _ = lax.optimization_barrier((codes[:quad], (other_codes, other_centered)))
    near_parts, near_sent = partial_sums(near_codes)
    own, near = pair_sums(near_parts, near_sent)
    summed = own + to_chip(near.astype(jnp.bfloat16), 2).astype(jnp.float32)
    for k, one in enumerate(far, 2):
        summed = summed + to_chip(one, 2 * k).astype(jnp.float32)
    row_error = (summed - centered[:rows_here].astype(jnp.float32)).astype(jnp.bfloat16)

    row_error, other_codes, other_centered = lax.optimization_barrier(
        (row_error, other_codes, other_centered)
    )
    blocks = in_turn(*gather_chips(row_error, chips))
    errors = jnp.concatenate(blocks, 0)
    other_errors = [to_other_core(jnp.concatenate(one, 0)) for one in (blocks[:4], blocks[4:])]
    totals = own_totals(codes[:, :latents_here].T, centered, errors, decoder)
    (
        encoder_next,
        encoder_moment_next,
        encoder_square_next,
        decoder_next,
        decoder_moment_next,
        decoder_square_next,
    ) = update(
        total_rows,
        other_codes.T,
        other_centered,
        other_errors,
        (encoder, decoder),
        (encoder_moment, encoder_square, decoder_moment, decoder_square),
        totals,
    )
    return (
        row_error,
        encoder_next,
        decoder_next,
        encoder_moment_next,
        encoder_square_next,
        decoder_moment_next,
        decoder_square_next,
    )


def solution(mesh):
    sharded = P(("groups", "latent"), None)
    return jax.shard_map(
        body,
        mesh=mesh,
        in_specs=(
            sharded,
            sharded,
            P(("groups", "latent")),
            sharded,
            P("groups"),
            sharded,
            sharded,
            sharded,
            sharded,
        ),
        out_specs=(sharded,) * 7,
        check_vma=False,
    )
```

```python
import functools

import jax
import jax.numpy as jnp
from jax import lax
from jax.experimental import pallas as pl
from jax.experimental.pallas import tpu as pltpu
from jax.sharding import PartitionSpec as P

beta_first = 0.9
beta_second = 0.999
step_rate = 0.001
adam_epsilon = 1e-08


def inner_last(left, right):
    return lax.dot_general(
        left, right, (((1,), (1,)), ((), ())), preferred_element_type=jnp.float32
    )


def by_parity(placed, errors, block):
    count = placed.shape[0] // block
    blocks = [(one, at) for one in errors for at in range(0, one.shape[0], block)]
    for k, (one, at) in enumerate(blocks):
        place = k // 2 + k % 2 * (count // 2)
        placed[pl.ds(place * block, block), :] = one[pl.ds(at, block), :]


def own_kernel(
    columns, block, codes_across, centered, sent, decoder, encoder_total, decoder_total, errors
):
    by_parity(errors, [sent], block)
    codes_t = codes_across[...]
    signal = inner_last(decoder[...], errors[...])
    delta_t = jnp.where(codes_t.astype(jnp.float32) > 0, signal, 0.0).astype(jnp.bfloat16)
    for start in range(0, decoder.shape[1], columns):
        at = pl.ds(start, columns)
        decoder_total[:, at] = jnp.dot(
            codes_t, errors[:, at], preferred_element_type=jnp.float32
        )
        encoder_total[:, at] = jnp.dot(
            delta_t, centered[:, at], preferred_element_type=jnp.float32
        )


def own_totals(codes_across, centered, errors, decoder, block):
    latents, width = decoder.shape
    rows = centered.shape[0]
    vmem = pl.BlockSpec(memory_space=pltpu.VMEM)
    total = jax.ShapeDtypeStruct((latents, width), jnp.float32)
    return pl.pallas_call(
        functools.partial(own_kernel, columns_of(width), block),
        out_shape=(total, total),
        in_specs=[vmem] * 4,
        out_specs=[vmem] * 2,
        scratch_shapes=[pltpu.VMEM((rows, width), jnp.bfloat16)],
        compiler_params=pltpu.CompilerParams(vmem_limit_bytes=16 * 1024 * 1024 + 8 * rows * width),
        cost_estimate=pl.CostEstimate(
            flops=6 * latents * width * rows,
            bytes_accessed=12 * latents * width + 4 * rows * width,
            transcendentals=0,
        ),
        name="own_totals",
    )(codes_across, centered, errors, decoder)


def columns_of(width):
    return next(c for c in (256, 128, width) if width % c == 0)


def update_kernel(columns, block, rows_total, codes_across, centered, *refs):
    blocks = len(refs) - 22
    errors, (encoder, decoder) = refs[:blocks], refs[blocks : blocks + 2]
    moments = refs[blocks + 2 : blocks + 6]
    totals = refs[blocks + 6 : blocks + 8]
    outs = refs[blocks + 8 : blocks + 14]
    error_all, *held, sem = refs[blocks + 14 :]
    tiles = encoder.shape[1] // columns
    part = min(32, encoder.shape[0])

    def write(t, i):
        at = pl.ds(t * columns, columns)
        return pltpu.make_async_copy(held[i].at[:, at], outs[i].at[:, at], sem.at[t, i])

    by_parity(error_all, errors, block)
    first = (1.0 - beta_first) / rows_total
    second = (1.0 - beta_second) / (rows_total * rows_total)

    def advance(which, left, right, weight):
        for t in range(tiles):
            at = pl.ds(t * columns, columns)
            total = jnp.dot(left, right[:, at], preferred_element_type=jnp.float32)
            for start in range(0, total.shape[0], part):
                some = (pl.ds(start, part), at)
                grad = totals[which][some] + total[start : start + part]
                moment = beta_first * moments[2 * which][some] + first * grad
                square = beta_second * moments[2 * which + 1][some] + second * (grad * grad)
                root = square * lax.rsqrt(square)
                held[3 * which][some] = (
                    weight[some].astype(jnp.float32)
                    - step_rate * moment * pl.reciprocal(root + adam_epsilon, approx=True)
                ).astype(jnp.bfloat16)
                held[3 * which + 1][some] = moment
                held[3 * which + 2][some] = square
            for i in range(3 * which, 3 * which + 3):
                write(t, i).start()

    codes_t = codes_across[...]
    advance(1, codes_t, error_all, decoder)
    signal = inner_last(decoder[...], error_all[...])
    delta_t = jnp.where(codes_t.astype(jnp.float32) > 0, signal, 0.0).astype(jnp.bfloat16)
    advance(0, delta_t, centered, encoder)
    for t in range(tiles):
        for i in range(6):
            write(t, i).wait()


def update(total_rows, codes_across, centered, errors, block, weights, moments, totals):
    latents, width = weights[0].shape
    rows = centered.shape[0]
    columns = columns_of(width)
    full = jax.ShapeDtypeStruct((latents, width), jnp.float32)
    half = jax.ShapeDtypeStruct((latents, width), jnp.bfloat16)
    vmem = pl.BlockSpec(memory_space=pltpu.VMEM)
    wide = pltpu.VMEM((latents, width), jnp.float32)
    narrow = pltpu.VMEM((latents, width), jnp.bfloat16)
    return pl.pallas_call(
        functools.partial(update_kernel, columns, block, float(total_rows)),
        out_shape=(half, full, full, half, full, full),
        in_specs=[vmem] * (len(errors) + 10),
        out_specs=[pl.BlockSpec(memory_space=pl.ANY)] * 6,
        scratch_shapes=[
            pltpu.VMEM((rows, width), jnp.bfloat16),
            narrow,
            wide,
            wide,
            narrow,
            wide,
            wide,
            pltpu.SemaphoreType.DMA((width // columns, 6)),
        ],
        compiler_params=pltpu.CompilerParams(vmem_limit_bytes=20 * 1024 * 1024 + 8 * rows * width),
        cost_estimate=pl.CostEstimate(
            flops=6 * latents * width * rows,
            bytes_accessed=44 * latents * width,
            transcendentals=4 * latents * width,
        ),
        name="update",
    )(codes_across, centered, *errors, *weights, *moments, *totals)


def to_chip(block, distance):
    size = lax.axis_size("latent")
    return lax.ppermute(
        block, "latent", [(i, i ^ (2 * distance)) for i in range(size)]
    )


def to_other_core(block):
    size = lax.axis_size("latent")
    return lax.ppermute(block, "latent", [(i, i ^ 1) for i in range(size)])


def gather_chips(block, chips):
    even = [block] + [to_chip(block, k) for k in range(2, chips, 2)]
    return even, [to_chip(one, 1) for one in even]


def in_turn(even, odd):
    return [one for both in zip(even, odd) for one in both]


def body(
    activations,
    encoder,
    encoder_bias,
    decoder,
    decoder_bias,
    encoder_moment,
    encoder_square,
    decoder_moment,
    decoder_square,
):
    rows_here, width = activations.shape
    latents_here = encoder.shape[0]
    size = lax.axis_size("latent")
    chips = size // 2
    total_rows = rows_here * size

    even, odd = gather_chips(activations, chips)
    rows_core = jnp.concatenate(even + odd, 0)
    encoder_both = jnp.concatenate([encoder, to_other_core(encoder)], 0)
    decoder_both = jnp.concatenate([decoder, to_other_core(decoder)], 0)
    bias_both = jnp.concatenate([encoder_bias, to_other_core(encoder_bias)], 0)

    centered = (rows_core.astype(jnp.float32) - decoder_bias).astype(jnp.bfloat16)
    codes = jnp.maximum(inner_last(centered, encoder_both) + bias_both, 0.0).astype(
        jnp.bfloat16
    )
    other_codes = to_other_core(codes[:, latents_here:])

    split, half = 2 * rows_here, chips // 2 * rows_here
    given = jnp.dot(codes[half:], decoder_both, preferred_element_type=jnp.float32).astype(
        jnp.bfloat16
    )

    def pair_sums(first, last, sent):
        return jnp.dot(
            codes[first:last], decoder_both, preferred_element_type=jnp.float32
        ) + to_chip(sent, 1).astype(jnp.float32)

    far_sent = given[split:]
    far = pair_sums(split, half, far_sent).astype(jnp.bfloat16)
    later_centered, _ = lax.optimization_barrier((centered, far_sent))
    other_centered = to_other_core(later_centered)
    near_sent, _ = lax.optimization_barrier((given[:split], (other_codes, other_centered)))
    near = pair_sums(0, split, near_sent)
    summed = near[:rows_here] + to_chip(near[rows_here:].astype(jnp.bfloat16), 2).astype(
        jnp.float32
    )
    for k in range(2, chips // 2):
        block = far[(k - 2) * rows_here : (k - 1) * rows_here]
        summed = summed + to_chip(block, 2 * k).astype(jnp.float32)
    row_error = (summed - centered[:rows_here].astype(jnp.float32)).astype(jnp.bfloat16)

    row_error, other_codes, other_centered = lax.optimization_barrier(
        (row_error, other_codes, other_centered)
    )
    blocks = in_turn(*gather_chips(row_error, chips))
    errors = jnp.concatenate(blocks, 0)
    other_errors = [to_other_core(jnp.concatenate(one, 0)) for one in (blocks[:4], blocks[4:])]
    totals = own_totals(codes[:, :latents_here].T, centered, errors, decoder, rows_here)
    (
        encoder_next,
        encoder_moment_next,
        encoder_square_next,
        decoder_next,
        decoder_moment_next,
        decoder_square_next,
    ) = update(
        total_rows,
        other_codes.T,
        other_centered,
        other_errors,
        rows_here,
        (encoder, decoder),
        (encoder_moment, encoder_square, decoder_moment, decoder_square),
        totals,
    )
    return (
        row_error,
        encoder_next,
        decoder_next,
        encoder_moment_next,
        encoder_square_next,
        decoder_moment_next,
        decoder_square_next,
    )


def solution(mesh):
    sharded = P(("groups", "latent"), None)
    return jax.shard_map(
        body,
        mesh=mesh,
        in_specs=(
            sharded,
            sharded,
            P(("groups", "latent")),
            sharded,
            P("groups"),
            sharded,
            sharded,
            sharded,
            sharded,
        ),
        out_specs=(sharded,) * 7,
        check_vma=False,
    )
```

```python
import functools

import jax
import jax.numpy as jnp
from jax import lax
from jax.experimental import pallas as pl
from jax.experimental.pallas import tpu as pltpu
from jax.sharding import PartitionSpec as P

beta_first = 0.9
beta_second = 0.999
step_rate = 0.001
adam_epsilon = 1e-08


def inner_last(left, right):
    return lax.dot_general(
        left, right, (((1,), (1,)), ((), ())), preferred_element_type=jnp.float32
    )


def own_kernel(columns, codes_across, centered, errors, decoder, encoder_total, decoder_total):
    codes_t = codes_across[...]
    signal = inner_last(decoder[...], errors[...])
    delta_t = jnp.where(codes_t.astype(jnp.float32) > 0, signal, 0.0).astype(jnp.bfloat16)
    for start in range(0, decoder.shape[1], columns):
        at = pl.ds(start, columns)
        decoder_total[:, at] = jnp.dot(
            codes_t, errors[:, at], preferred_element_type=jnp.float32
        )
        encoder_total[:, at] = jnp.dot(
            delta_t, centered[:, at], preferred_element_type=jnp.float32
        )


def own_totals(codes_across, centered, errors, decoder):
    latents, width = decoder.shape
    rows = centered.shape[0]
    vmem = pl.BlockSpec(memory_space=pltpu.VMEM)
    total = jax.ShapeDtypeStruct((latents, width), jnp.float32)
    return pl.pallas_call(
        functools.partial(own_kernel, columns_of(width)),
        out_shape=(total, total),
        in_specs=[vmem] * 4,
        out_specs=[vmem] * 2,
        compiler_params=pltpu.CompilerParams(vmem_limit_bytes=16 * 1024 * 1024 + 8 * rows * width),
        cost_estimate=pl.CostEstimate(
            flops=6 * latents * width * rows,
            bytes_accessed=12 * latents * width + 4 * rows * width,
            transcendentals=0,
        ),
        name="own_totals",
    )(codes_across, centered, errors, decoder)


def columns_of(width):
    return next(c for c in (256, 128, width) if width % c == 0)


def update_kernel(columns, rows_total, codes_across, centered, *refs):
    blocks = len(refs) - 22
    errors, (encoder, decoder) = refs[:blocks], refs[blocks : blocks + 2]
    moments = refs[blocks + 2 : blocks + 6]
    totals = refs[blocks + 6 : blocks + 8]
    outs = refs[blocks + 8 : blocks + 14]
    error_all, *held, sem = refs[blocks + 14 :]
    tiles = encoder.shape[1] // columns
    part = min(32, encoder.shape[0])

    def write(t, i):
        at = pl.ds(t * columns, columns)
        return pltpu.make_async_copy(held[i].at[:, at], outs[i].at[:, at], sem.at[t, i])

    start = 0
    for one in errors:
        error_all[pl.ds(start, one.shape[0]), :] = one[...]
        start += one.shape[0]
    first = (1.0 - beta_first) / rows_total
    second = (1.0 - beta_second) / (rows_total * rows_total)

    def advance(which, left, right, weight):
        for t in range(tiles):
            at = pl.ds(t * columns, columns)
            total = jnp.dot(left, right[:, at], preferred_element_type=jnp.float32)
            for start in range(0, total.shape[0], part):
                some = (pl.ds(start, part), at)
                grad = totals[which][some] + total[start : start + part]
                moment = beta_first * moments[2 * which][some] + first * grad
                square = beta_second * moments[2 * which + 1][some] + second * (grad * grad)
                root = square * lax.rsqrt(square)
                held[3 * which][some] = (
                    weight[some].astype(jnp.float32)
                    - step_rate * moment * pl.reciprocal(root + adam_epsilon, approx=True)
                ).astype(jnp.bfloat16)
                held[3 * which + 1][some] = moment
                held[3 * which + 2][some] = square
            for i in range(3 * which, 3 * which + 3):
                write(t, i).start()

    codes_t = codes_across[...]
    advance(1, codes_t, error_all, decoder)
    signal = inner_last(decoder[...], error_all[...])
    delta_t = jnp.where(codes_t.astype(jnp.float32) > 0, signal, 0.0).astype(jnp.bfloat16)
    advance(0, delta_t, centered, encoder)
    for t in range(tiles):
        for i in range(6):
            write(t, i).wait()


def update(total_rows, codes_across, centered, errors, weights, moments, totals):
    latents, width = weights[0].shape
    rows = centered.shape[0]
    columns = columns_of(width)
    full = jax.ShapeDtypeStruct((latents, width), jnp.float32)
    half = jax.ShapeDtypeStruct((latents, width), jnp.bfloat16)
    vmem = pl.BlockSpec(memory_space=pltpu.VMEM)
    wide = pltpu.VMEM((latents, width), jnp.float32)
    narrow = pltpu.VMEM((latents, width), jnp.bfloat16)
    return pl.pallas_call(
        functools.partial(update_kernel, columns, float(total_rows)),
        out_shape=(half, full, full, half, full, full),
        in_specs=[vmem] * (len(errors) + 10),
        out_specs=[pl.BlockSpec(memory_space=pl.ANY)] * 6,
        scratch_shapes=[
            pltpu.VMEM((rows, width), jnp.bfloat16),
            narrow,
            wide,
            wide,
            narrow,
            wide,
            wide,
            pltpu.SemaphoreType.DMA((width // columns, 6)),
        ],
        compiler_params=pltpu.CompilerParams(vmem_limit_bytes=20 * 1024 * 1024 + 8 * rows * width),
        cost_estimate=pl.CostEstimate(
            flops=6 * latents * width * rows,
            bytes_accessed=44 * latents * width,
            transcendentals=4 * latents * width,
        ),
        name="update",
    )(codes_across, centered, *errors, *weights, *moments, *totals)


def to_chip(block, distance):
    size = lax.axis_size("latent")
    return lax.ppermute(
        block, "latent", [(i, i ^ (2 * distance)) for i in range(size)]
    )


def to_other_core(block):
    size = lax.axis_size("latent")
    return lax.ppermute(block, "latent", [(i, i ^ 1) for i in range(size)])


def gather_chips(block, chips):
    even = [block] + [to_chip(block, k) for k in range(2, chips, 2)]
    return even, [to_chip(one, 1) for one in even]


def in_turn(even, odd):
    return [one for both in zip(even, odd) for one in both]


def body(
    activations,
    encoder,
    encoder_bias,
    decoder,
    decoder_bias,
    encoder_moment,
    encoder_square,
    decoder_moment,
    decoder_square,
):
    rows_here, width = activations.shape
    latents_here = encoder.shape[0]
    size = lax.axis_size("latent")
    chips = size // 2
    total_rows = rows_here * size

    even, odd = gather_chips(activations, chips)
    rows_core = jnp.concatenate(in_turn(even, odd), 0)
    sent, _ = lax.optimization_barrier(((encoder_bias, encoder, decoder), odd[1]))
    bias_both, encoder_both, decoder_both = (
        jnp.concatenate([mine, to_other_core(one)], 0)
        for mine, one in zip((encoder_bias, encoder, decoder), sent)
    )

    centered = (rows_core.astype(jnp.float32) - decoder_bias).astype(jnp.bfloat16)
    codes = jnp.maximum(inner_last(centered, encoder_both) + bias_both, 0.0).astype(
        jnp.bfloat16
    )
    other_codes = to_other_core(codes[:, latents_here:])

    quad = 4 * rows_here
    parts = []
    for rows in (slice(0, quad), slice(quad, None)):
        sums = jnp.dot(codes[rows], decoder_both, preferred_element_type=jnp.float32)
        parts += [sums[at : at + rows_here] for at in range(0, sums.shape[0], rows_here)]

    def given(first, last):
        return jnp.concatenate(parts[first + 1 : last : 2], 0).astype(jnp.bfloat16)

    def pair_sums(first, last, sent):
        came = to_chip(sent, 1)
        return [
            parts[k] + came[at * rows_here : (at + 1) * rows_here].astype(jnp.float32)
            for at, k in enumerate(range(first, last, 2))
        ]

    far_sent = given(4, chips)
    far = [one.astype(jnp.bfloat16) for one in pair_sums(4, chips, far_sent)]
    later_centered, _ = lax.optimization_barrier((centered, far_sent))
    other_centered = to_other_core(later_centered)
    near_sent, _ = lax.optimization_barrier((given(0, 4), (other_codes, other_centered)))
    own, near = pair_sums(0, 4, near_sent)
    summed = own + to_chip(near.astype(jnp.bfloat16), 2).astype(jnp.float32)
    for k, one in enumerate(far, 2):
        summed = summed + to_chip(one, 2 * k).astype(jnp.float32)
    row_error = (summed - centered[:rows_here].astype(jnp.float32)).astype(jnp.bfloat16)

    row_error, other_codes, other_centered = lax.optimization_barrier(
        (row_error, other_codes, other_centered)
    )
    blocks = in_turn(*gather_chips(row_error, chips))
    errors = jnp.concatenate(blocks, 0)
    other_errors = [to_other_core(jnp.concatenate(one, 0)) for one in (blocks[:4], blocks[4:])]
    totals = own_totals(codes[:, :latents_here].T, centered, errors, decoder)
    (
        encoder_next,
        encoder_moment_next,
        encoder_square_next,
        decoder_next,
        decoder_moment_next,
        decoder_square_next,
    ) = update(
        total_rows,
        other_codes.T,
        other_centered,
        other_errors,
        (encoder, decoder),
        (encoder_moment, encoder_square, decoder_moment, decoder_square),
        totals,
    )
    return (
        row_error,
        encoder_next,
        decoder_next,
        encoder_moment_next,
        encoder_square_next,
        decoder_moment_next,
        decoder_square_next,
    )


def solution(mesh):
    sharded = P(("groups", "latent"), None)
    return jax.shard_map(
        body,
        mesh=mesh,
        in_specs=(
            sharded,
            sharded,
            P(("groups", "latent")),
            sharded,
            P("groups"),
            sharded,
            sharded,
            sharded,
            sharded,
        ),
        out_specs=(sharded,) * 7,
        check_vma=False,
    )
```

```python
import functools

import jax
import jax.numpy as jnp
from jax import lax
from jax.experimental import pallas as pl
from jax.experimental.pallas import tpu as pltpu
from jax.sharding import PartitionSpec as P

beta_first = 0.9
beta_second = 0.999
step_rate = 0.001
adam_epsilon = 1e-08


def inner_last(left, right):
    return lax.dot_general(
        left, right, (((1,), (1,)), ((), ())), preferred_element_type=jnp.float32
    )


def place_blocks(placed, errors, block):
    pairs = (placed.shape[0] // block - 4) // 2
    blocks = [(one, at) for one in errors for at in range(0, one.shape[0], block)]
    for k, (one, at) in enumerate(blocks):
        place = k if k < 4 else 4 + 2 * (pairs - 1 - (k - 4) // 2) + k % 2
        placed[pl.ds(place * block, block), :] = one[pl.ds(at, block), :]


def own_kernel(
    columns, block, codes_across, centered, sent, decoder, encoder_total, decoder_total, errors
):
    place_blocks(errors, [sent], block)
    codes_t = codes_across[...]
    signal = inner_last(decoder[...], errors[...])
    delta_t = jnp.where(codes_t.astype(jnp.float32) > 0, signal, 0.0).astype(jnp.bfloat16)
    for start in range(0, decoder.shape[1], columns):
        at = pl.ds(start, columns)
        decoder_total[:, at] = jnp.dot(
            codes_t, errors[:, at], preferred_element_type=jnp.float32
        )
        encoder_total[:, at] = jnp.dot(
            delta_t, centered[:, at], preferred_element_type=jnp.float32
        )


def own_totals(codes_across, centered, errors, decoder, block):
    latents, width = decoder.shape
    rows = centered.shape[0]
    vmem = pl.BlockSpec(memory_space=pltpu.VMEM)
    total = jax.ShapeDtypeStruct((latents, width), jnp.float32)
    return pl.pallas_call(
        functools.partial(own_kernel, columns_of(width), block),
        out_shape=(total, total),
        in_specs=[vmem] * 4,
        out_specs=[vmem] * 2,
        scratch_shapes=[pltpu.VMEM((rows, width), jnp.bfloat16)],
        compiler_params=pltpu.CompilerParams(vmem_limit_bytes=16 * 1024 * 1024 + 8 * rows * width),
        cost_estimate=pl.CostEstimate(
            flops=6 * latents * width * rows,
            bytes_accessed=12 * latents * width + 4 * rows * width,
            transcendentals=0,
        ),
        name="own_totals",
    )(codes_across, centered, errors, decoder)


def columns_of(width):
    return next(c for c in (256, 128, width) if width % c == 0)


def update_kernel(columns, block, rows_total, codes_across, centered, *refs):
    blocks = len(refs) - 22
    errors, (encoder, decoder) = refs[:blocks], refs[blocks : blocks + 2]
    moments = refs[blocks + 2 : blocks + 6]
    totals = refs[blocks + 6 : blocks + 8]
    outs = refs[blocks + 8 : blocks + 14]
    error_all, *held, sem = refs[blocks + 14 :]
    tiles = encoder.shape[1] // columns
    part = min(32, encoder.shape[0])

    def write(t, i):
        at = pl.ds(t * columns, columns)
        return pltpu.make_async_copy(held[i].at[:, at], outs[i].at[:, at], sem.at[t, i])

    place_blocks(error_all, errors, block)
    first = (1.0 - beta_first) / rows_total
    second = (1.0 - beta_second) / (rows_total * rows_total)

    def advance(which, left, right, weight):
        for t in range(tiles):
            at = pl.ds(t * columns, columns)
            total = jnp.dot(left, right[:, at], preferred_element_type=jnp.float32)
            for start in range(0, total.shape[0], part):
                some = (pl.ds(start, part), at)
                grad = totals[which][some] + total[start : start + part]
                moment = beta_first * moments[2 * which][some] + first * grad
                square = beta_second * moments[2 * which + 1][some] + second * (grad * grad)
                root = square * lax.rsqrt(square)
                held[3 * which][some] = (
                    weight[some].astype(jnp.float32)
                    - step_rate * moment * pl.reciprocal(root + adam_epsilon, approx=True)
                ).astype(jnp.bfloat16)
                held[3 * which + 1][some] = moment
                held[3 * which + 2][some] = square
            for i in range(3 * which, 3 * which + 3):
                write(t, i).start()

    codes_t = codes_across[...]
    advance(1, codes_t, error_all, decoder)
    signal = inner_last(decoder[...], error_all[...])
    delta_t = jnp.where(codes_t.astype(jnp.float32) > 0, signal, 0.0).astype(jnp.bfloat16)
    advance(0, delta_t, centered, encoder)
    for t in range(tiles):
        for i in range(6):
            write(t, i).wait()


def update(total_rows, codes_across, centered, errors, block, weights, moments, totals):
    latents, width = weights[0].shape
    rows = centered.shape[0]
    columns = columns_of(width)
    full = jax.ShapeDtypeStruct((latents, width), jnp.float32)
    half = jax.ShapeDtypeStruct((latents, width), jnp.bfloat16)
    vmem = pl.BlockSpec(memory_space=pltpu.VMEM)
    wide = pltpu.VMEM((latents, width), jnp.float32)
    narrow = pltpu.VMEM((latents, width), jnp.bfloat16)
    return pl.pallas_call(
        functools.partial(update_kernel, columns, block, float(total_rows)),
        out_shape=(half, full, full, half, full, full),
        in_specs=[vmem] * (len(errors) + 10),
        out_specs=[pl.BlockSpec(memory_space=pl.ANY)] * 6,
        scratch_shapes=[
            pltpu.VMEM((rows, width), jnp.bfloat16),
            narrow,
            wide,
            wide,
            narrow,
            wide,
            wide,
            pltpu.SemaphoreType.DMA((width // columns, 6)),
        ],
        compiler_params=pltpu.CompilerParams(vmem_limit_bytes=20 * 1024 * 1024 + 8 * rows * width),
        cost_estimate=pl.CostEstimate(
            flops=6 * latents * width * rows,
            bytes_accessed=44 * latents * width,
            transcendentals=4 * latents * width,
        ),
        name="update",
    )(codes_across, centered, *errors, *weights, *moments, *totals)


def to_chip(block, distance):
    size = lax.axis_size("latent")
    return lax.ppermute(
        block, "latent", [(i, i ^ (2 * distance)) for i in range(size)]
    )


def to_other_core(block):
    size = lax.axis_size("latent")
    return lax.ppermute(block, "latent", [(i, i ^ 1) for i in range(size)])


def gather_chips(block, chips):
    even = [block] + [to_chip(block, k) for k in range(2, chips, 2)]
    return even, [to_chip(one, 1) for one in even]


def in_turn(even, odd):
    return [one for both in zip(even, odd) for one in both]


def body(
    activations,
    encoder,
    encoder_bias,
    decoder,
    decoder_bias,
    encoder_moment,
    encoder_square,
    decoder_moment,
    decoder_square,
):
    rows_here, width = activations.shape
    latents_here = encoder.shape[0]
    size = lax.axis_size("latent")
    chips = size // 2
    total_rows = rows_here * size

    even, odd = gather_chips(activations, chips)
    blocks = in_turn(even, odd)
    for k in range(chips - 2, 2, -2):
        blocks += blocks[k : k + 2]
    rows_core = jnp.concatenate(blocks[:4] + blocks[chips:], 0)
    sent, _ = lax.optimization_barrier(((encoder_bias, encoder, decoder), odd[1]))
    bias_both, encoder_both, decoder_both = (
        jnp.concatenate([mine, to_other_core(one)], 0)
        for mine, one in zip((encoder_bias, encoder, decoder), sent)
    )

    centered = (rows_core.astype(jnp.float32) - decoder_bias).astype(jnp.bfloat16)
    codes = jnp.maximum(inner_last(centered, encoder_both) + bias_both, 0.0).astype(
        jnp.bfloat16
    )
    other_codes = to_other_core(codes[:, latents_here:])

    quad = 4 * rows_here
    parts = []
    for rows in (slice(0, quad), slice(quad, None)):
        sums = jnp.dot(codes[rows], decoder_both, preferred_element_type=jnp.float32)
        parts += [sums[at : at + rows_here] for at in range(0, sums.shape[0], rows_here)]

    def given(first, last):
        return jnp.concatenate(parts[first + 1 : last : 2], 0).astype(jnp.bfloat16)

    def pair_sums(first, last, sent):
        came = to_chip(sent, 1)
        return [
            parts[k] + came[at * rows_here : (at + 1) * rows_here].astype(jnp.float32)
            for at, k in enumerate(range(first, last, 2))
        ]

    far_sent = given(4, chips)
    far = [one.astype(jnp.bfloat16) for one in pair_sums(4, chips, far_sent)]
    later_centered, _ = lax.optimization_barrier((centered, far_sent))
    other_centered = to_other_core(later_centered)
    near_sent, _ = lax.optimization_barrier((given(0, 4), (other_codes, other_centered)))
    own, near = pair_sums(0, 4, near_sent)
    summed = own + to_chip(near.astype(jnp.bfloat16), 2).astype(jnp.float32)
    for k, one in enumerate(far):
        summed = summed + to_chip(one, chips - 2 - 2 * k).astype(jnp.float32)
    row_error = (summed - centered[:rows_here].astype(jnp.float32)).astype(jnp.bfloat16)

    row_error, other_codes, other_centered = lax.optimization_barrier(
        (row_error, other_codes, other_centered)
    )
    blocks = in_turn(*gather_chips(row_error, chips))
    errors = jnp.concatenate(blocks, 0)
    other_errors = [to_other_core(jnp.concatenate(one, 0)) for one in (blocks[:4], blocks[4:])]
    totals = own_totals(codes[:, :latents_here].T, centered, errors, decoder, rows_here)
    (
        encoder_next,
        encoder_moment_next,
        encoder_square_next,
        decoder_next,
        decoder_moment_next,
        decoder_square_next,
    ) = update(
        total_rows,
        other_codes.T,
        other_centered,
        other_errors,
        rows_here,
        (encoder, decoder),
        (encoder_moment, encoder_square, decoder_moment, decoder_square),
        totals,
    )
    return (
        row_error,
        encoder_next,
        decoder_next,
        encoder_moment_next,
        encoder_square_next,
        decoder_moment_next,
        decoder_square_next,
    )


def solution(mesh):
    sharded = P(("groups", "latent"), None)
    return jax.shard_map(
        body,
        mesh=mesh,
        in_specs=(
            sharded,
            sharded,
            P(("groups", "latent")),
            sharded,
            P("groups"),
            sharded,
            sharded,
            sharded,
            sharded,
        ),
        out_specs=(sharded,) * 7,
        check_vma=False,
    )
```

```python
import functools

import jax
import jax.numpy as jnp
from jax import lax
from jax.experimental import pallas as pl
from jax.experimental.pallas import tpu as pltpu
from jax.sharding import PartitionSpec as P

beta_first = 0.9
beta_second = 0.999
step_rate = 0.001
adam_epsilon = 1e-08


def inner_last(left, right):
    return lax.dot_general(
        left, right, (((1,), (1,)), ((), ())), preferred_element_type=jnp.float32
    )


def own_kernel(columns, codes_across, centered, errors, decoder, encoder_total, decoder_total):
    codes_t = codes_across[...]
    signal = inner_last(decoder[...], errors[...])
    delta_t = jnp.where(codes_t.astype(jnp.float32) > 0, signal, 0.0).astype(jnp.bfloat16)
    for start in range(0, decoder.shape[1], columns):
        at = pl.ds(start, columns)
        decoder_total[:, at] = jnp.dot(
            codes_t, errors[:, at], preferred_element_type=jnp.float32
        )
        encoder_total[:, at] = jnp.dot(
            delta_t, centered[:, at], preferred_element_type=jnp.float32
        )


def own_totals(codes_across, centered, errors, decoder):
    latents, width = decoder.shape
    rows = centered.shape[0]
    vmem = pl.BlockSpec(memory_space=pltpu.VMEM)
    total = jax.ShapeDtypeStruct((latents, width), jnp.float32)
    return pl.pallas_call(
        functools.partial(own_kernel, columns_of(width)),
        out_shape=(total, total),
        in_specs=[vmem] * 4,
        out_specs=[vmem] * 2,
        compiler_params=pltpu.CompilerParams(vmem_limit_bytes=16 * 1024 * 1024 + 8 * rows * width),
        cost_estimate=pl.CostEstimate(
            flops=6 * latents * width * rows,
            bytes_accessed=12 * latents * width + 4 * rows * width,
            transcendentals=0,
        ),
        name="own_totals",
    )(codes_across, centered, errors, decoder)


def columns_of(width):
    return next(c for c in (256, 128, width) if width % c == 0)


def update_kernel(columns, rows_total, codes_across, centered, *refs):
    blocks = len(refs) - 22
    errors, (encoder, decoder) = refs[:blocks], refs[blocks : blocks + 2]
    moments = refs[blocks + 2 : blocks + 6]
    totals = refs[blocks + 6 : blocks + 8]
    outs = refs[blocks + 8 : blocks + 14]
    error_all, *held, sem = refs[blocks + 14 :]
    tiles = encoder.shape[1] // columns
    part = min(32, encoder.shape[0])

    def write(t, i):
        at = pl.ds(t * columns, columns)
        return pltpu.make_async_copy(held[i].at[:, at], outs[i].at[:, at], sem.at[t, i])

    start = 0
    for one in errors:
        error_all[pl.ds(start, one.shape[0]), :] = one[...]
        start += one.shape[0]
    first = (1.0 - beta_first) / rows_total
    second = (1.0 - beta_second) / (rows_total * rows_total)

    def advance(which, left, right, weight):
        for t in range(tiles):
            at = pl.ds(t * columns, columns)
            total = jnp.dot(left, right[:, at], preferred_element_type=jnp.float32)
            for start in range(0, total.shape[0], part):
                some = (pl.ds(start, part), at)
                grad = totals[which][some] + total[start : start + part]
                moment = beta_first * moments[2 * which][some] + first * grad
                square = beta_second * moments[2 * which + 1][some] + second * (grad * grad)
                root = square * lax.rsqrt(square)
                held[3 * which][some] = (
                    weight[some].astype(jnp.float32)
                    - step_rate * moment * pl.reciprocal(root + adam_epsilon, approx=True)
                ).astype(jnp.bfloat16)
                held[3 * which + 1][some] = moment
                held[3 * which + 2][some] = square
            for i in range(3 * which, 3 * which + 3):
                write(t, i).start()

    codes_t = codes_across[...]
    advance(1, codes_t, error_all, decoder)
    signal = inner_last(decoder[...], error_all[...])
    delta_t = jnp.where(codes_t.astype(jnp.float32) > 0, signal, 0.0).astype(jnp.bfloat16)
    advance(0, delta_t, centered, encoder)
    for t in range(tiles):
        for i in range(6):
            write(t, i).wait()


def update(total_rows, codes_across, centered, errors, weights, moments, totals):
    latents, width = weights[0].shape
    rows = centered.shape[0]
    columns = columns_of(width)
    full = jax.ShapeDtypeStruct((latents, width), jnp.float32)
    half = jax.ShapeDtypeStruct((latents, width), jnp.bfloat16)
    vmem = pl.BlockSpec(memory_space=pltpu.VMEM)
    wide = pltpu.VMEM((latents, width), jnp.float32)
    narrow = pltpu.VMEM((latents, width), jnp.bfloat16)
    return pl.pallas_call(
        functools.partial(update_kernel, columns, float(total_rows)),
        out_shape=(half, full, full, half, full, full),
        in_specs=[vmem] * (len(errors) + 10),
        out_specs=[pl.BlockSpec(memory_space=pl.ANY)] * 6,
        scratch_shapes=[
            pltpu.VMEM((rows, width), jnp.bfloat16),
            narrow,
            wide,
            wide,
            narrow,
            wide,
            wide,
            pltpu.SemaphoreType.DMA((width // columns, 6)),
        ],
        compiler_params=pltpu.CompilerParams(vmem_limit_bytes=20 * 1024 * 1024 + 8 * rows * width),
        cost_estimate=pl.CostEstimate(
            flops=6 * latents * width * rows,
            bytes_accessed=44 * latents * width,
            transcendentals=4 * latents * width,
        ),
        name="update",
    )(codes_across, centered, *errors, *weights, *moments, *totals)


def to_chip(block, distance):
    size = lax.axis_size("latent")
    return lax.ppermute(
        block, "latent", [(i, i ^ (2 * distance)) for i in range(size)]
    )


def to_other_core(block):
    size = lax.axis_size("latent")
    return lax.ppermute(block, "latent", [(i, i ^ 1) for i in range(size)])


def gather_chips(block, chips):
    even = [block] + [to_chip(block, k) for k in range(2, chips, 2)]
    return even, [to_chip(one, 1) for one in even]


def in_turn(even, odd):
    return [one for both in zip(even, odd) for one in both]


def body(
    activations,
    encoder,
    encoder_bias,
    decoder,
    decoder_bias,
    encoder_moment,
    encoder_square,
    decoder_moment,
    decoder_square,
):
    rows_here, width = activations.shape
    latents_here = encoder.shape[0]
    size = lax.axis_size("latent")
    chips = size // 2
    total_rows = rows_here * size

    rows_core = jnp.concatenate(in_turn(*gather_chips(activations, chips)), 0)
    encoder_both = jnp.concatenate([encoder, to_other_core(encoder)], 0)
    decoder_both = jnp.concatenate([decoder, to_other_core(decoder)], 0)
    bias_both = jnp.concatenate([encoder_bias, to_other_core(encoder_bias)], 0)

    centered = (rows_core.astype(jnp.float32) - decoder_bias).astype(jnp.bfloat16)
    codes = jnp.maximum(inner_last(centered, encoder_both) + bias_both, 0.0).astype(
        jnp.bfloat16
    )
    other_codes = to_other_core(codes[:, latents_here:])

    quad = 4 * rows_here

    def partial_sums(some_codes):
        sums = jnp.dot(some_codes, decoder_both, preferred_element_type=jnp.float32)
        parts = [sums[at : at + rows_here] for at in range(0, sums.shape[0], rows_here)]
        return parts, jnp.concatenate(parts[1::2], 0).astype(jnp.bfloat16)

    def pair_sums(parts, sent):
        came = to_chip(sent, 1)
        return [
            part + came[at * rows_here : (at + 1) * rows_here].astype(jnp.float32)
            for at, part in enumerate(parts[::2])
        ]

    far_parts, far_sent = partial_sums(codes[quad:])
    far = [one.astype(jnp.bfloat16) for one in pair_sums(far_parts, far_sent)]
    later_centered, _ = lax.optimization_barrier((centered, far_sent))
    other_centered = to_other_core(later_centered)
    near_codes, _ = lax.optimization_barrier((codes[:quad], (other_codes, other_centered)))
    near_parts, near_sent = partial_sums(near_codes)
    own, near = pair_sums(near_parts, near_sent)
    summed = own + to_chip(near.astype(jnp.bfloat16), 2).astype(jnp.float32)
    for k, one in enumerate(far, 2):
        summed = summed + to_chip(one, 2 * k).astype(jnp.float32)
    row_error = (summed - centered[:rows_here].astype(jnp.float32)).astype(jnp.bfloat16)

    row_error, other_codes, other_centered = lax.optimization_barrier(
        (row_error, other_codes, other_centered)
    )
    blocks = in_turn(*gather_chips(row_error, chips))
    errors = jnp.concatenate(blocks, 0)
    other_errors = [
        to_other_core(jnp.concatenate(one, 0)) for one in (blocks[:3], blocks[3:4], blocks[4:])
    ]
    totals = own_totals(codes[:, :latents_here].T, centered, errors, decoder)
    (
        encoder_next,
        encoder_moment_next,
        encoder_square_next,
        decoder_next,
        decoder_moment_next,
        decoder_square_next,
    ) = update(
        total_rows,
        other_codes.T,
        other_centered,
        other_errors,
        (encoder, decoder),
        (encoder_moment, encoder_square, decoder_moment, decoder_square),
        totals,
    )
    return (
        row_error,
        encoder_next,
        decoder_next,
        encoder_moment_next,
        encoder_square_next,
        decoder_moment_next,
        decoder_square_next,
    )


def solution(mesh):
    sharded = P(("groups", "latent"), None)
    return jax.shard_map(
        body,
        mesh=mesh,
        in_specs=(
            sharded,
            sharded,
            P(("groups", "latent")),
            sharded,
            P("groups"),
            sharded,
            sharded,
            sharded,
            sharded,
        ),
        out_specs=(sharded,) * 7,
        check_vma=False,
    )
```
